32 devices in a mesh: arc: 2 (over core), row: 2 (over x), col: 8 (over z, y).
Axes of the slice: x: 2, y: 2, z: 4, core: 2. Of those that a mesh axis runs over, the one named last changes fastest.
Arguments:
- design: bfloat16 [6144, 6, 8, 128], P(('arc', 'row'), None, 'col'), may hold values from -0.076546554 to 0.076546554
- obs_weight: float32 [6144], P(('arc', 'row')), may hold values from 0.25 to 4
- prior: float32 [6, 8, 128], P(None, 'col'), may hold values from 0.3 to 3
Outputs:
- normal: float32 [24, 2, 128, 6, 8, 128], P(None, 'row', None, None, 'col')
- panel: float32 [24, 2, 128, 1024], P(None, 'row')
The draws below stay inside these ranges and needn't reach their ends.
All inputs are finite; a program needn't handle non-finite values.
Results may differ from the reference program's by a relative error of at most 0.0012.
Values may be sent and summed in bfloat16 or wider, within the bound.
No kernel may reach another device: no remote copies, remote signals or barrier semaphores. Data moves between devices by JAX's collectives and lax.ppermute only.
A program may use at most 128 MiB of HBM per device.

```python
import math
import jax
import jax.numpy as jnp
from jax import lax

K = 6144
PW = 1024
ROWS = 6144
TB = 128
KC = 6
KT_R = 24
N_ROW = 2
N_COL = 8


def draw_design(key, part):
    key = jax.random.fold_in(key, 11)
    noise_key, common_key, loading_key = jax.random.split(key, 3)
    group_width = 64
    groups = K // group_width
    factor = 0.8 * float(ROWS) ** (-0.5)
    noise = jnp.clip(jax.random.normal(noise_key, (ROWS, groups, group_width), jnp.float32), -4.0, 4.0)
    common = jnp.clip(jax.random.normal(common_key, (ROWS, groups, 1), jnp.float32), -3.0, 3.0)
    loading = jax.random.uniform(loading_key, (1, groups, group_width), jnp.float32, 0.4, 0.8)
    values = (noise + loading * common) * factor
    return values.reshape(ROWS, KC, N_COL, TB).astype(jnp.bfloat16)


def level_of(key, dims, cuts, least, largest):
    def one(position, shards_of):
        draws = jax.random.uniform(jax.random.fold_in(jax.random.fold_in(key, 6), position), (shards_of,), jnp.float32, least / len(cuts), largest / len(cuts))
        return jnp.repeat(jnp.exp(draws), dims[position] // shards_of).reshape((-1,) + (1,) * (len(dims) - position - 1))

    gain = one(*cuts[0])
    for cut in cuts[1:]:
        gain = gain * one(*cut)
    return gain


def setup_inputs(seed: int = 0) -> dict:
    key_of = jax.random.split(jax.random.key(seed), 4)
    design = draw_design(jax.random.fold_in(key_of[3], 71), 0)
    obs_weight = jnp.clip(jnp.exp(math.log(4.0) - 2.7725887 * jax.random.uniform(key_of[1], (ROWS,), jnp.float32) ** level_of(key_of[1], (ROWS,), ((0, 4),), -0.2, 0.2)), 0.25, 4.0)
    prior = jnp.clip(jnp.exp(math.log(3.0) - 2.3025851 * jax.random.uniform(key_of[2], (KC, N_COL, TB), jnp.float32) ** level_of(key_of[2], (KC, N_COL, TB), ((1, 8),), -0.2, 0.2)), 0.3, 3.0)
    return dict(design=design, obs_weight=obs_weight, prior=prior)


def reference(design, obs_weight, prior):
    rows = design.shape[0]
    flat = design.reshape(rows, K)
    weighted = (flat.astype(jnp.float32) * obs_weight[:, None]).astype(jnp.bfloat16)
    gram = jnp.dot(flat.astype(jnp.float32).T.astype(jnp.float32), weighted.astype(jnp.float32), precision=lax.Precision.HIGHEST, preferred_element_type=jnp.float32)
    gram = gram + jnp.diag(prior.reshape(K))
    normal = gram.reshape(KT_R, N_ROW, TB, KC, N_COL, TB)
    factor = jnp.linalg.cholesky(gram[:PW, :PW])
    panel = lax.linalg.triangular_solve(factor, gram[:, :PW], left_side=False, lower=True, transpose_a=True)
    return (normal, panel.reshape(KT_R, N_ROW, TB, PW))
```

```python
import jax
import jax.numpy as jnp
from jax import lax
from jax.sharding import PartitionSpec as P

F32 = jnp.float32
BF16 = jnp.bfloat16


def ring_order(n):
    return list(range(0, n, 2)) + list(range(1, n, 2))[::-1]


def swap(x, axis, shift=1):
    n = lax.axis_size(axis)
    return lax.ppermute(x, axis, [(i, (i + shift) % n) for i in range(n)])


def gather_cols(x):
    n = lax.axis_size("col")
    order = ring_order(n)
    got = lax.all_gather(x, "col", axis=0, tiled=False, axis_index_groups=[order])
    return jnp.stack([got[order.index(c)] for c in range(n)])


def partial_sums(blocks, weights):
    n_row = lax.axis_size("row")
    r = lax.axis_index("row")
    by_owner = blocks.reshape((blocks.shape[0] // n_row, n_row) + blocks.shape[1:])

    def part(owner):
        mine = lax.dynamic_index_in_dim(by_owner, owner, 1, keepdims=False)
        return jnp.einsum("q...rt,jru->q...tju", mine, weights, preferred_element_type=F32)

    arrived = [
        swap(part((r + d) % n_row).astype(BF16), "row", d) for d in range(1, n_row)
    ]
    total = part(r)
    for x in arrived:
        total = total + x.astype(F32)
    return total


def body(design, obs_weight, prior):
    n_row = lax.axis_size("row")
    n_col = lax.axis_size("col")
    a = lax.axis_index("arc")
    r = lax.axis_index("row")
    c = lax.axis_index("col")
    rows, kc, _, t = design.shape
    q = n_col // n_row
    m = (kc - 1) // 2
    own = jnp.transpose(design[:, :, 0, :], (1, 0, 2))
    lead_own = gather_cols(own[0])
    priors = gather_cols(prior[0, 0])
    rest_own = gather_cols(own[1 + 2 * m :])
    other = swap(own, "arc")
    weight_other = swap(obs_weight, "arc")

    def weigh(x, w):
        return (x.astype(F32) * w[:, None]).astype(BF16)

    both_own = jnp.concatenate([own, other], axis=1)
    w2 = jnp.concatenate([obs_weight, weight_other])
    weighted = weigh(both_own, w2)
    share = lax.dynamic_slice_in_dim(both_own, 1 + m * a, m, 0)

    lead = jnp.concatenate([lead_own, swap(lead_own, "arc")], axis=1)
    lead_weighted = weigh(lead, w2)
    half = n_col // 2
    lead_half = lax.dynamic_slice_in_dim(lead, half * a, half, 0)
    square_half = jnp.einsum("crt,jru->ctju", lead_half, lead_weighted, preferred_element_type=F32)
    for_sum = square_half
    if n_row == 2:
        square_half = square_half + swap(for_sum, "row")
    else:
        square_half = lax.psum(for_sum, "row")
    square_other = swap(square_half, "arc")
    first = a == 0
    square = jnp.concatenate(
        [jnp.where(first, square_half, square_other), jnp.where(first, square_other, square_half)]
    )
    width = n_col * t
    square = square.reshape(width, width) + jnp.diag(priors.reshape(width))

    main = gather_cols(share)
    rest = jnp.concatenate([rest_own, swap(rest_own, "arc")], axis=2)
    rest_half = lax.dynamic_slice_in_dim(rest, half * a, half, 0)

    def whole(main_rows, half_rows):
        main_rows = jnp.swapaxes(main_rows, 0, 1)
        other_main = swap(main_rows, "arc")
        other_half = swap(half_rows, "arc")

        def in_order(x, y):
            return jnp.where(first, x, y), jnp.where(first, y, x)

        lo, hi = in_order(main_rows, other_main)
        halves = jnp.swapaxes(jnp.concatenate(in_order(half_rows, other_half), axis=0), 0, 1)
        return halves, lo, hi

    halved = jnp.concatenate([lead_half[:, None], rest_half], axis=1)
    n_main = partial_sums(main, weighted)
    n_half = partial_sums(halved, weighted)
    halves, lo, hi = whole(n_main, n_half)
    tiles = jnp.concatenate([halves[:1], lo, hi, halves[1:]], axis=0)
    tiles = tiles.reshape(kc * q, t, kc, t)
    tile_rows = jnp.arange(kc * q, dtype=jnp.int32) * n_row + r
    tile_cols = jnp.arange(kc, dtype=jnp.int32) * n_col + c
    same = (tile_rows[:, None] == tile_cols[None, :]).astype(F32)
    identity = jnp.eye(t, dtype=F32)
    added = same[:, None, :, None] * identity[None, :, None, :] * prior.reshape(kc, t)[None, None]
    normal = (tiles + added).reshape(kc * q, 1, t, kc, 1, t)

    p_main = partial_sums(main, lead_weighted)
    p_half = partial_sums(rest_half, lead_weighted)
    halves, lo, hi = whole(p_main, p_half)
    top = lax.dynamic_index_in_dim(square.reshape(q, n_row, t, width), r, 1, keepdims=False)
    panel_rows = jnp.concatenate(
        [top[None].reshape(1, q, t, width)]
        + [x.reshape(-1, q, t, width) for x in (lo, hi, halves)],
        axis=0,
    ).reshape(kc * q * t, width)
    factor = jnp.linalg.cholesky(square)
    result = lax.linalg.triangular_solve(
        factor, panel_rows, left_side=False, lower=True, transpose_a=True
    )
    return (normal, result.reshape(kc * q, 1, t, width))


def solution(mesh):
    placed = (P(("arc", "row"), None, "col", None), P(("arc", "row")), P(None, "col", None))
    return jax.shard_map(
        body,
        mesh=mesh,
        in_specs=placed,
        out_specs=(P(None, "row", None, None, "col", None), P(None, "row", None, None)),
        check_vma=False,
    )
```

```python
import functools

import jax
import jax.numpy as jnp
from jax import lax
from jax.experimental import pallas as pl
from jax.experimental.pallas import tpu as pltpu
from jax.sharding import PartitionSpec as P

F32 = jnp.float32
BF16 = jnp.bfloat16

BLOCK = 128
STRIP = 16


def dot_tn(x, y):
    return lax.dot_general(
        x, y, (((0,), (0,)), ((), ())), precision=lax.Precision.HIGHEST, preferred_element_type=F32
    )


def dot_nn(x, y):
    return jnp.dot(x, y, precision=lax.Precision.HIGHEST, preferred_element_type=F32)


def inverse_factor(square):
    n = square.shape[0]
    count = n // STRIP
    row_id = lax.broadcasted_iota(jnp.int32, (STRIP, n), 0)
    left = [square[i * STRIP : (i + 1) * STRIP, :] for i in range(count)]
    lane = lax.broadcasted_iota(jnp.int32, (STRIP, n), 1)
    right = [(lane == row_id + i * STRIP).astype(F32) for i in range(count)]
    done = []
    for b in range(count):
        ps, pe = left[b], right[b]
        columns = [
            jnp.broadcast_to(ps[:, b * STRIP + l : b * STRIP + l + 1], (STRIP, n))
            for l in range(STRIP)
        ]
        scale = jnp.zeros((STRIP, n), F32)
        for j in range(STRIP):
            rs = lax.rsqrt(columns[j][j : j + 1, :])
            col = columns[j] * rs
            below = jnp.where(row_id > j, col, 0.0)
            ps = ps - below * (ps[j : j + 1, :] * rs)
            pe = pe - below * (pe[j : j + 1, :] * rs)
            for l in range(j + 1, STRIP):
                columns[l] = columns[l] - col * (columns[l][j : j + 1, :] * rs)
            scale = jnp.where(row_id == j, rs, scale)
        ps = ps * scale
        pe = pe * scale
        done.append(pe)
        if b + 1 < count:
            update = dot_tn(ps, jnp.concatenate([ps, pe], axis=1))
            for i in range(b + 1, count):
                left[i] = left[i] - update[i * STRIP : (i + 1) * STRIP, :n]
                right[i] = right[i] - update[i * STRIP : (i + 1) * STRIP, n:]
    return jnp.concatenate(done, axis=0)


def factor_step(k, blocks, s_ref, *refs):
    lo, hi = k * BLOCK, (k + 1) * BLOCK
    if k:
        u_ref, e_ref, u_out, e_out = refs
        above = u_ref[:, lo:hi]
        diag = s_ref[:, lo:hi] - dot_tn(above, above)
    else:
        u_out, e_out = refs
        diag = s_ref[:, lo:hi]
    inverse = inverse_factor(diag)
    width = blocks * BLOCK
    u_out[:, :hi] = jnp.zeros((BLOCK, hi), F32)
    if k + 1 < blocks:
        rest = s_ref[:, hi:]
        if k:
            rest = rest - dot_tn(above, u_ref[:, hi:])
        u_out[:, hi:] = dot_nn(inverse, rest)
        e_out[:, hi:] = jnp.zeros((BLOCK, width - hi), F32)
    if k:
        e_out[:, :lo] = -dot_nn(inverse, dot_tn(above, e_ref[:, :lo]))
    e_out[:, lo:hi] = inverse


def inverse_cholesky_steps(square, ahead):
    width = square.shape[0]
    blocks = width // BLOCK
    shape = jax.ShapeDtypeStruct((width, width), F32)
    state = None
    for k in range(blocks):
        if k in ahead:
            state, _ = lax.optimization_barrier((state, ahead[k]))
        row = pl.BlockSpec((BLOCK, width), lambda i, k=k: (k, 0))
        seen = pl.BlockSpec((k * BLOCK, width), lambda i: (0, 0))
        state = pl.pallas_call(
            functools.partial(factor_step, k, blocks),
            grid=(1,),
            out_shape=(shape, shape),
            in_specs=[row] + ([seen, seen] if k else []),
            out_specs=(row, row),
            input_output_aliases={1: 0, 2: 1} if k else {},
            compiler_params=pltpu.CompilerParams(vmem_limit_bytes=40 * 1024 * 1024),
            cost_estimate=pl.CostEstimate(flops=10**7, bytes_accessed=36 * 10**6, transcendentals=0),
            name=f"factor_{k}",
        )(square, *(state or ()))
        yield state


def ring_order(n, owners):
    order = []
    for owner in range(owners):
        order += list(range(owner, n, owners))[:: -1 if owner % 2 else 1]
    return order


def swap(x, axis, shift=1):
    n = lax.axis_size(axis)
    return lax.ppermute(x, axis, [(i, (i + shift) % n) for i in range(n)])


def gather_cols(x, order):
    return lax.all_gather(x, "col", axis=0, tiled=False, axis_index_groups=[order])


def weigh(x, w):
    return (x.astype(F32) * w[:, None]).astype(BF16)


def split3(x):
    hi = lax.reduce_precision(x, 8, 7)
    mid = lax.reduce_precision(x - hi, 8, 7)
    return [y.astype(BF16) for y in (hi, mid, x - hi - mid)]


def by_owner(x):
    n_row = lax.axis_size("row")
    return x.reshape((n_row, x.shape[0] // n_row) + x.shape[1:])


def partial_sums(blocks, *weights):
    n_row = lax.axis_size("row")
    r = lax.axis_index("row")

    def part(owner, w):
        mine = lax.dynamic_index_in_dim(blocks, owner, 0, keepdims=False)
        return jnp.einsum("qrt,ru->qtu", mine, w, preferred_element_type=F32)

    sent = [[part((r + d) % n_row, w).astype(BF16) for d in range(1, n_row)] for w in weights]
    totals = []
    for w, parts in zip(weights, sent):
        arrived = [swap(x, "row", 1 + i) for i, x in enumerate(parts)]
        total = part(r, w)
        for x in arrived:
            total = total + x.astype(F32)
        totals.append(total)
    return totals, sent


def half_of(x):
    half = x.shape[1] // 2
    return lax.dynamic_slice_in_dim(x, half * lax.axis_index("arc"), half, 1)


PAIRS = (((0, 0), (0, 1), (0, 2), (0, 3), (3, 3)), ((1, 1), (1, 2), (1, 3), (2, 2), (2, 3)))
WIDE = 256


def lead_kernel(order, rows, pairs_ref, own_ref, other_ref, w_ref, weighted_ref, s_ref, flat_ref):
    @pl.when(pl.program_id(0) == 0)
    def _():
        t = own_ref.shape[2]
        for pos, c in enumerate(order):
            for arc, ref in enumerate((own_ref, other_ref)):
                x = ref[pos, :rows, :]
                place = (pl.ds(arc * rows, rows), pl.ds(c * t, t))
                flat_ref[place] = x
                weighted_ref[place] = (x.astype(F32) * w_ref[pl.ds(arc * rows, rows), :]).astype(BF16)

    def columns(entry):
        return pl.ds(pl.multiple_of(pairs_ref[2 * pl.program_id(0) + entry] * WIDE, WIDE), WIDE)

    def product(x, y):
        return lax.dot_general(x, y, (((0,), (0,)), ((), ())), preferred_element_type=F32)

    i, j = columns(0), columns(1)
    s_ref[0] = 0.5 * (
        product(flat_ref[:, i], weighted_ref[:, j]) + product(weighted_ref[:, i], flat_ref[:, j])
    )


def lead_blocks(own, other, w2, order, rows):
    n, padded, t = own.shape
    width = n * t
    count = len(PAIRS[0])
    pairs = jnp.array(PAIRS, jnp.int32).reshape(2, 2 * count)[lax.axis_index("arc")]
    whole = pl.BlockSpec((n, padded, t), lambda s, p: (0, 0, 0))
    return pl.pallas_call(
        functools.partial(lead_kernel, order, rows),
        grid_spec=pltpu.PrefetchScalarGridSpec(
            num_scalar_prefetch=1,
            grid=(count,),
            in_specs=[whole, whole, pl.BlockSpec((2 * rows, t), lambda s, p: (0, 0))],
            out_specs=(
                pl.BlockSpec((2 * rows, width), lambda s, p: (0, 0)),
                pl.BlockSpec((1, WIDE, WIDE), lambda s, p: (s, 0, 0)),
            ),
            scratch_shapes=[pltpu.VMEM((2 * rows, width), BF16)],
        ),
        out_shape=(
            jax.ShapeDtypeStruct((2 * rows, width), BF16),
            jax.ShapeDtypeStruct((count, WIDE, WIDE), F32),
        ),
        compiler_params=pltpu.CompilerParams(vmem_limit_bytes=52 * 1024 * 1024),
        cost_estimate=pl.CostEstimate(flops=4 * 10**9, bytes_accessed=14 * 10**6, transcendentals=0),
        name="lead_blocks",
    )(pairs, own, other, jnp.broadcast_to(w2[:, None], (2 * rows, t)))


def assemble_kernel(table_ref, mine_ref, theirs_ref, prior_ref, out_ref):
    i, j = pl.program_id(0), pl.program_id(1)
    entry = table_ref[4 * i + j]
    block = jnp.where(entry < 8, mine_ref[entry % 8], theirs_ref[entry % 8])

    @pl.when(i < j)
    def _():
        out_ref[...] = block

    @pl.when(i > j)
    def _():
        out_ref[...] = block.T

    @pl.when(i == j)
    def _():
        x = lax.broadcasted_iota(jnp.int32, block.shape, 0)
        y = lax.broadcasted_iota(jnp.int32, block.shape, 1)
        out_ref[...] = block + jnp.where(x == y, prior_ref[...], 0.0)


def assemble(mine, theirs, priors):
    width = priors.shape[0]
    tables = [[0] * 16, [0] * 16]
    for core in range(2):
        for slot, (i, j) in enumerate(PAIRS[core]):
            for a in range(2):
                tables[a][4 * i + j] = tables[a][4 * j + i] = slot + (0 if a == core else 8)
    table = jnp.array(tables, jnp.int32)[lax.axis_index("arc")]
    blocks = pl.BlockSpec(mine.shape, lambda i, j, p: (0, 0, 0))
    return pl.pallas_call(
        assemble_kernel,
        grid_spec=pltpu.PrefetchScalarGridSpec(
            num_scalar_prefetch=1,
            grid=(4, 4),
            in_specs=[blocks, blocks, pl.BlockSpec((1, WIDE), lambda i, j, p: (0, j))],
            out_specs=pl.BlockSpec((WIDE, WIDE), lambda i, j, p: (i, j)),
        ),
        out_shape=jax.ShapeDtypeStruct((width, width), F32),
        compiler_params=pltpu.CompilerParams(vmem_limit_bytes=24 * 1024 * 1024),
        cost_estimate=pl.CostEstimate(flops=10**6, bytes_accessed=7 * 10**6, transcendentals=0),
        name="assemble",
    )(table, mine, theirs, priors[None])


def finish_kernel(top, halved, kc, q, n_row, base, step, here_ref, *refs):
    if top:
        n_mine, n_theirs, square_ref, hi_ref, lo_ref, prior_ref = refs[:6]
    else:
        n_mine, n_theirs, p_mine, p_theirs, hi_ref, lo_ref, prior_ref = refs[:7]
    normal_ref, panel_ref, phi, plo = refs[-4:]
    a, r, c = here_ref[0], here_ref[1], here_ref[2]
    g = pl.program_id(0)
    t = prior_ref.shape[1]
    k = base + step * g
    x = lax.broadcasted_iota(jnp.int32, (t, t), 0)
    y = lax.broadcasted_iota(jnp.int32, (t, t), 1)
    for z in range(q):
        at = jnp.where(r % 2 == 1, q - 1 - z, z)
        core, index = (at // (q // 2), at % (q // 2)) if halved else (g, at)
        use = core == a
        rows = jnp.where(use, n_mine[index], n_theirs[index])
        for k2 in range(kc):
            tile = rows[:, k2 * t : (k2 + 1) * t]
            same = jnp.logical_and(k == k2, c == z * n_row + r)
            tile = tile + jnp.where(jnp.logical_and(same, x == y), prior_ref[k2 : k2 + 1, :], 0.0)
            normal_ref[pl.ds(z * t * kc + k2, t, stride=kc), :] = tile
        if top:
            first = pl.multiple_of((z * n_row + r) * t, t)
            rows = square_ref[pl.ds(first, t), :]
        else:
            rows = jnp.where(use, p_mine[index], p_theirs[index])
        high = rows.astype(BF16)
        phi[z * t : (z + 1) * t, :] = high
        plo[z * t : (z + 1) * t, :] = (rows - high.astype(F32)).astype(BF16)

    def product(u, v):
        return lax.dot_general(u, v, (((1,), (1,)), ((), ())), preferred_element_type=F32)

    width = panel_ref.shape[1]
    for lo in range(0, width, WIDE):
        hi = lo + WIDE
        panel_ref[:, lo:hi] = (
            product(phi[:, :hi], hi_ref[lo:hi, :hi])
            + product(phi[:, :hi], lo_ref[lo:hi, :hi])
            + product(plo[:, :hi], hi_ref[lo:hi, :hi])
        )


def finish(outputs, here, n_rows, p_rows, inverse, prior, halved, base, step, count, kc, q, n_row):
    t = prior.shape[1]
    width = inverse[0].shape[0]
    top = len(p_rows) == 1
    arrays = [*n_rows, *p_rows, *inverse, prior]

    def whole(x):
        return pl.BlockSpec(x.shape, lambda g, p: (0,) * x.ndim)

    shapes = (
        jax.ShapeDtypeStruct((kc * q * t * kc, t), F32),
        jax.ShapeDtypeStruct((kc * q * t, width), F32),
    )
    n_in = 1 + len(arrays)
    return pl.pallas_call(
        functools.partial(finish_kernel, top, halved, kc, q, n_row, base, step),
        grid_spec=pltpu.PrefetchScalarGridSpec(
            num_scalar_prefetch=1,
            grid=(count,),
            in_specs=[whole(x) for x in arrays] + [pl.BlockSpec(memory_space=pl.ANY)] * len(outputs),
            out_specs=(
                pl.BlockSpec((q * t * kc, t), lambda g, p: (base + step * g, 0)),
                pl.BlockSpec((q * t, width), lambda g, p: (base + step * g, 0)),
            ),
            scratch_shapes=[pltpu.VMEM((q * t, width), BF16)] * 2,
        ),
        out_shape=shapes,
        input_output_aliases={n_in: 0, n_in + 1: 1} if outputs else {},
        compiler_params=pltpu.CompilerParams(vmem_limit_bytes=52 * 1024 * 1024),
        cost_estimate=pl.CostEstimate(
            flops=count * 2 * 10**9, bytes_accessed=count * 8 * 10**6, transcendentals=0
        ),
        name=f"finish_{base}",
    )(here, *arrays, *outputs)


def body(design, obs_weight, prior):
    n_row = lax.axis_size("row")
    n_col = lax.axis_size("col")
    a = lax.axis_index("arc")
    r = lax.axis_index("row")
    c = lax.axis_index("col")
    rows, kc, _, t = design.shape
    q = n_col // n_row
    m = (kc - 1) // 2
    width = n_col * t
    first = a == 0
    fast = t == 128 and width == 4 * WIDE
    order = ring_order(n_col, n_row)
    own = jnp.transpose(design[:, :, 0, :], (1, 0, 2))

    extra = jnp.concatenate([p[None] for p in split3(prior[0, 0])] + [jnp.zeros((13, t), BF16)])
    lead_own = gather_cols(jnp.concatenate([own[0], extra]), order)
    other = swap(own, "arc")
    weight_other = swap(obs_weight, "arc")
    both = jnp.concatenate([own, other], axis=1)
    w2 = jnp.concatenate([obs_weight, weight_other])
    weighted = jnp.transpose(weigh(both, w2), (1, 0, 2)).reshape(2 * rows, kc * t)
    weighted = lax.optimization_barrier(weighted)
    share = lax.dynamic_slice_in_dim(both, 1 + m * a, m, 0)
    main = [gather_cols(share[i], order) for i in range(m)]
    lead_own, later = lax.optimization_barrier((lead_own, own[1 + 2 * m :]))
    rest_own = [gather_cols(x, order) for x in later]
    lead_other = swap(lead_own, "arc")
    priors = jnp.sum(lead_own[:, rows : rows + 3].astype(F32), axis=1)
    priors = jnp.concatenate([priors[order.index(x)] for x in range(n_col)])

    if fast:
        lead_weighted, packed = lead_blocks(lead_own, lead_other, w2, order, rows)
        arrived = swap(packed, "row")
        lead_own, lead_other, packed = lax.optimization_barrier((lead_own, lead_other, packed))
        packed = packed + arrived
        symmetric = assemble(packed, swap(packed, "arc"), priors)
    else:
        flat = jnp.concatenate([lead_own[:, :rows], lead_other[:, :rows]], axis=1)
        flat = jnp.stack([flat[order.index(x)] for x in range(n_col)])
        lead_weighted = jnp.transpose(weigh(flat, w2), (1, 0, 2)).reshape(2 * rows, width)
        half = n_col // 2
        square = jnp.einsum(
            "crt,ru->ctu",
            lax.dynamic_slice_in_dim(flat, half * a, half, 0),
            lead_weighted,
            preferred_element_type=F32,
        )
        square = lax.psum(square, "row")
        square_other = swap(square, "arc")
        square = jnp.concatenate(
            [jnp.where(first, square, square_other), jnp.where(first, square_other, square)]
        ).reshape(width, width)
        symmetric = 0.5 * (square + square.T) + jnp.diag(priors)

    lead = half_of(by_owner(jnp.concatenate([lead_own[:, :rows], lead_other[:, :rows]], axis=1)))
    n_lead, _ = partial_sums(lead, weighted)
    main_sums = [partial_sums(by_owner(x), weighted, lead_weighted) for x in main]

    steps = inverse_cholesky_steps(symmetric, {3: main_sums[0][1]} if fast else {})
    *_, (_, inverse) = steps

    rest_sums = []
    for x in rest_own:
        x = half_of(by_owner(jnp.concatenate([x, swap(x, "arc")], axis=1)))
        rest_sums.append(partial_sums(x, weighted, lead_weighted))

    def pair(x):
        return [x, swap(x, "arc")]

    if fast:
        high = lax.reduce_precision(inverse, 8, 7)
        inverse = (high.astype(BF16), (inverse - high).astype(BF16))
        here = jnp.stack([a, r, c]).astype(jnp.int32)
        prior = prior.reshape(kc, t)
        shape = (kc, q, n_row)
        out = finish([], here, pair(n_lead[0]), [symmetric], inverse, prior, True, 0, 1, 1, *shape)
        for i, ((n, p), _) in enumerate(main_sums):
            out = finish(out, here, pair(n), pair(p), inverse, prior, False, 1 + i, m, 2, *shape)
        for i, ((n, p), _) in enumerate(rest_sums):
            out = finish(out, here, pair(n), pair(p), inverse, prior, True, 1 + 2 * m + i, 1, 1, *shape)
        normal, panel = out
        return (normal.reshape(kc * q, 1, t, kc, 1, t), panel.reshape(kc * q, 1, t, width))

    def sides(x):
        y = swap(x, "arc")
        return jnp.where(first, x, y), jnp.where(first, y, x)

    n_rows, p_rows = [None] * kc, [None] * kc
    n_rows[0] = jnp.concatenate(sides(n_lead[0]))
    for i, ((n, p), _) in enumerate(main_sums):
        n_rows[1 + i], n_rows[1 + m + i] = sides(n)
        p_rows[1 + i], p_rows[1 + m + i] = sides(p)
    for i, ((n, p), _) in enumerate(rest_sums):
        n_rows[1 + 2 * m + i] = jnp.concatenate(sides(n))
        p_rows[1 + 2 * m + i] = jnp.concatenate(sides(p))

    def in_order(x):
        x = jnp.stack(x)
        return jnp.where(r % 2 == 1, x[:, ::-1], x)

    tiles = in_order(n_rows).reshape(kc * q, t, kc, t)
    tile_rows = jnp.arange(kc * q, dtype=jnp.int32) * n_row + r
    tile_cols = jnp.arange(kc, dtype=jnp.int32) * n_col + c
    same = (tile_rows[:, None] == tile_cols[None, :]).astype(F32)
    identity = jnp.eye(t, dtype=F32)
    added = same[:, None, :, None] * identity[None, :, None, :] * prior.reshape(kc, t)[None, None]
    normal = (tiles + added).reshape(kc * q, 1, t, kc, 1, t)
    top = lax.dynamic_index_in_dim(symmetric.reshape(q, n_row, t, width), r, 1, keepdims=False)
    panel_rows = jnp.concatenate([top[None], in_order(p_rows[1:])])
    result = jnp.einsum(
        "rk,jk->rj",
        panel_rows.reshape(kc * q * t, width),
        inverse,
        precision=lax.Precision.HIGH,
        preferred_element_type=F32,
    )
    return (normal, result.reshape(kc * q, 1, t, width))


def solution(mesh):
    placed = (P(("arc", "row"), None, "col", None), P(("arc", "row")), P(None, "col", None))
    return jax.shard_map(
        body,
        mesh=mesh,
        in_specs=placed,
        out_specs=(P(None, "row", None, None, "col", None), P(None, "row", None, None)),
        check_vma=False,
    )
```

```python
import functools

import jax
import jax.numpy as jnp
from jax import lax
from jax.experimental import pallas as pl
from jax.experimental.pallas import tpu as pltpu
from jax.sharding import PartitionSpec as P

F32 = jnp.float32
BF16 = jnp.bfloat16

SHORT = pl.CostEstimate(flops=10**6, bytes_accessed=10**5, transcendentals=0)
BLOCK = 128
STRIP = 16


def dot_tn(x, y):
    return lax.dot_general(
        x, y, (((0,), (0,)), ((), ())), precision=lax.Precision.HIGHEST, preferred_element_type=F32
    )


def dot_nn(x, y):
    return jnp.dot(x, y, precision=lax.Precision.HIGHEST, preferred_element_type=F32)


def inverse_factor(square):
    n = square.shape[0]
    count = n // STRIP
    row_id = lax.broadcasted_iota(jnp.int32, (STRIP, n), 0)
    left = [square[i * STRIP : (i + 1) * STRIP, :] for i in range(count)]
    lane = lax.broadcasted_iota(jnp.int32, (STRIP, n), 1)
    right = [(lane == row_id + i * STRIP).astype(F32) for i in range(count)]
    done = []
    for b in range(count):
        ps, pe = left[b], right[b]
        columns = [
            jnp.broadcast_to(ps[:, b * STRIP + l : b * STRIP + l + 1], (STRIP, n))
            for l in range(STRIP)
        ]
        scale = jnp.zeros((STRIP, n), F32)
        for j in range(STRIP):
            rs = lax.rsqrt(columns[j][j : j + 1, :])
            col = columns[j] * rs
            below = jnp.where(row_id > j, col, 0.0)
            ps = ps - below * (ps[j : j + 1, :] * rs)
            pe = pe - below * (pe[j : j + 1, :] * rs)
            for l in range(j + 1, STRIP):
                columns[l] = columns[l] - col * (columns[l][j : j + 1, :] * rs)
            scale = jnp.where(row_id == j, rs, scale)
        ps = ps * scale
        pe = pe * scale
        done.append(pe)
        if b + 1 < count:
            update = dot_tn(ps, jnp.concatenate([ps, pe], axis=1))
            for i in range(b + 1, count):
                left[i] = left[i] - update[i * STRIP : (i + 1) * STRIP, :n]
                right[i] = right[i] - update[i * STRIP : (i + 1) * STRIP, n:]
    return jnp.concatenate(done, axis=0)


def factor_step(k, blocks, s_ref, *refs):
    lo, hi = k * BLOCK, (k + 1) * BLOCK
    u_out, e_out, high_out, low_out = refs[-4:]
    if k:
        u_ref, e_ref = refs[:2]
        above = u_ref[:, lo:hi]
        diag = s_ref[:, lo:hi] - dot_tn(above, above)
    else:
        diag = s_ref[:, lo:hi]
    inverse = inverse_factor(diag)
    width = blocks * BLOCK
    u_out[:, :hi] = jnp.zeros((BLOCK, hi), F32)
    if k + 1 < blocks:
        rest = s_ref[:, hi:]
        if k:
            rest = rest - dot_tn(above, u_ref[:, hi:])
        u_out[:, hi:] = dot_nn(inverse, rest)
        e_out[:, hi:] = jnp.zeros((BLOCK, width - hi), F32)
    if k:
        e_out[:, :lo] = -dot_nn(inverse, dot_tn(above, e_ref[:, :lo]))
    e_out[:, lo:hi] = inverse
    rows = e_out[...]
    high = rows.astype(BF16)
    high_out[...] = high
    low_out[...] = (rows - high.astype(F32)).astype(BF16)


def inverse_cholesky_steps(square, ahead):
    width = square.shape[0]
    blocks = width // BLOCK
    shape = jax.ShapeDtypeStruct((width, width), F32)
    part = jax.ShapeDtypeStruct((width, width), BF16)
    held = pl.BlockSpec(memory_space=pl.ANY)
    state = None
    for k in range(blocks):
        gates = []
        if k in ahead:
            gate = after(jnp.zeros((1,), jnp.int32), *ahead[k])
            gates = [gate]
        row = pl.BlockSpec((BLOCK, width), lambda i, k=k: (k, 0))
        seen = pl.BlockSpec((k * BLOCK, width), lambda i: (0, 0))
        state = pl.pallas_call(
            functools.partial(factor_step, k, blocks),
            grid=(1,),
            out_shape=(shape, shape, part, part),
            in_specs=[row]
            + ([seen, seen, held, held] if k else [])
            + [pl.BlockSpec(memory_space=pltpu.SMEM)] * len(gates),
            out_specs=(row, row, row, row),
            input_output_aliases={1 + i: i for i in range(4)} if k else {},
            compiler_params=pltpu.CompilerParams(vmem_limit_bytes=40 * 1024 * 1024),
            cost_estimate=SHORT,
            name=f"factor_{k}",
        )(square, *(state or ()), *gates)
        yield state


def ring_order(n, owners):
    order = []
    for owner in range(owners):
        order += list(range(owner, n, owners))[:: -1 if owner % 2 else 1]
    return order


def swap(x, axis, shift=1):
    n = lax.axis_size(axis)
    return lax.ppermute(x, axis, [(i, (i + shift) % n) for i in range(n)])


def after(index, *others):
    for x in others:
        one = lax.slice(x, (0,) * x.ndim, (1,) * x.ndim).reshape(()).astype(F32)
        index = index + jnp.minimum(jnp.abs(one), 0.0).astype(jnp.int32)
    return index


def gather_cols(x, order):
    return lax.all_gather(x, "col", axis=0, tiled=False, axis_index_groups=[order])


def weigh(x, w):
    return (x.astype(F32) * w[:, None]).astype(BF16)


def split3(x):
    hi = lax.reduce_precision(x, 8, 7)
    mid = lax.reduce_precision(x - hi, 8, 7)
    return [y.astype(BF16) for y in (hi, mid, x - hi - mid)]


def by_owner(x):
    n_row = lax.axis_size("row")
    return x.reshape((n_row, x.shape[0] // n_row) + x.shape[1:])


def product_of(blocks, owner, group):
    total = 0.0
    for x, w in zip(blocks, group):
        mine = lax.dynamic_index_in_dim(x, owner, 0, keepdims=False)
        total += jnp.einsum("qrt,ru->qtu", mine, w, preferred_element_type=F32)
    return total


def sends(blocks, groups, *wait):
    n_row = lax.axis_size("row")
    r = after(lax.axis_index("row"), *wait)
    parts = [
        [product_of(blocks, (r + d) % n_row, w).astype(BF16) for d in range(1, n_row)]
        for w in groups
    ]
    return lax.optimization_barrier(parts)


def keeps(blocks, groups, *wait):
    r = after(lax.axis_index("row"), *wait)
    return lax.optimization_barrier([product_of(blocks, r, w) for w in groups])


def receive(sent):
    return [[swap(x, "row", 1 + i) for i, x in enumerate(parts)] for parts in sent]


def partial_sums(blocks, *groups):
    totals = []
    for total, parts in zip(keeps(blocks, groups), receive(sends(blocks, groups))):
        for x in parts:
            total = total + x.astype(F32)
        totals.append(total)
    return totals


def core_half(x, core):
    half = x.shape[1] // 2
    return lax.dynamic_slice_in_dim(x, half * core, half, 1)


def core_halves(x):
    a = lax.axis_index("arc")
    return [core_half(x, a), swap(core_half(x, 1 - a), "arc")]


PAIRS = (((0, 0), (0, 1), (0, 2), (0, 3), (3, 3)), ((1, 1), (1, 2), (1, 3), (2, 2), (2, 3)))
WIDE = 256


def lead_kernel(order, rows, pairs_ref, own_ref, other_ref, w_ref, weighted_ref, s_ref, flat_ref):
    @pl.when(pl.program_id(0) == 0)
    def _():
        t = own_ref.shape[2]
        for pos, c in enumerate(order):
            for arc, ref in enumerate((own_ref, other_ref)):
                x = ref[pos, :rows, :]
                place = (pl.ds(arc * rows, rows), pl.ds(c * t, t))
                flat_ref[place] = x
                weighted_ref[place] = (x.astype(F32) * w_ref[pl.ds(arc * rows, rows), :]).astype(BF16)

    def columns(entry):
        return pl.ds(pl.multiple_of(pairs_ref[2 * pl.program_id(0) + entry] * WIDE, WIDE), WIDE)

    def product(x, y):
        return lax.dot_general(x, y, (((0,), (0,)), ((), ())), preferred_element_type=F32)

    i, j = columns(0), columns(1)
    s_ref[0] = 0.5 * (
        product(flat_ref[:, i], weighted_ref[:, j]) + product(weighted_ref[:, i], flat_ref[:, j])
    )


def lead_blocks(own, other, w2, order, rows, *wait):
    n, padded, t = own.shape
    width = n * t
    count = len(PAIRS[0])
    pairs = jnp.array(PAIRS, jnp.int32).reshape(2, 2 * count)[lax.axis_index("arc")]
    pairs = after(pairs, *wait)
    whole = pl.BlockSpec((n, padded, t), lambda s, p: (0, 0, 0))
    return pl.pallas_call(
        functools.partial(lead_kernel, order, rows),
        grid_spec=pltpu.PrefetchScalarGridSpec(
            num_scalar_prefetch=1,
            grid=(count,),
            in_specs=[whole, whole, pl.BlockSpec((2 * rows, t), lambda s, p: (0, 0))],
            out_specs=(
                pl.BlockSpec((2 * rows, width), lambda s, p: (0, 0)),
                pl.BlockSpec((1, WIDE, WIDE), lambda s, p: (s, 0, 0)),
            ),
            scratch_shapes=[pltpu.VMEM((2 * rows, width), BF16)],
        ),
        out_shape=(
            jax.ShapeDtypeStruct((2 * rows, width), BF16),
            jax.ShapeDtypeStruct((count, WIDE, WIDE), F32),
        ),
        compiler_params=pltpu.CompilerParams(vmem_limit_bytes=52 * 1024 * 1024),
        cost_estimate=SHORT,
        name="lead_blocks",
    )(pairs, own, other, jnp.broadcast_to(w2[:, None], (2 * rows, t)))


def assemble_kernel(table_ref, mine_ref, theirs_ref, late_ref, late_other_ref, prior_ref, out_ref):
    i, j = pl.program_id(0), pl.program_id(1)
    entry = table_ref[4 * i + j]
    at = entry % 8
    block = jnp.where(entry < 8, mine_ref[at] + late_ref[at], theirs_ref[at] + late_other_ref[at])

    @pl.when(i < j)
    def _():
        out_ref[...] = block

    @pl.when(i > j)
    def _():
        out_ref[...] = block.T

    @pl.when(i == j)
    def _():
        x = lax.broadcasted_iota(jnp.int32, block.shape, 0)
        y = lax.broadcasted_iota(jnp.int32, block.shape, 1)
        out_ref[...] = block + jnp.where(x == y, prior_ref[...], 0.0)


def assemble(mine, theirs, late, late_other, priors, *wait):
    width = priors.shape[0]
    tables = [[0] * 16, [0] * 16]
    for core in range(2):
        for slot, (i, j) in enumerate(PAIRS[core]):
            for a in range(2):
                tables[a][4 * i + j] = tables[a][4 * j + i] = slot + (0 if a == core else 8)
    table = after(jnp.array(tables, jnp.int32)[lax.axis_index("arc")], *wait)
    blocks = pl.BlockSpec(mine.shape, lambda i, j, p: (0, 0, 0))
    return pl.pallas_call(
        assemble_kernel,
        grid_spec=pltpu.PrefetchScalarGridSpec(
            num_scalar_prefetch=1,
            grid=(4, 4),
            in_specs=[blocks] * 4 + [pl.BlockSpec((1, WIDE), lambda i, j, p: (0, j))],
            out_specs=pl.BlockSpec((WIDE, WIDE), lambda i, j, p: (i, j)),
        ),
        out_shape=jax.ShapeDtypeStruct((width, width), F32),
        compiler_params=pltpu.CompilerParams(vmem_limit_bytes=24 * 1024 * 1024),
        cost_estimate=SHORT,
        name="assemble",
    )(table, mine, theirs, late, late_other, priors[None])


def finish_kernel(top, halved, kc, q, n_row, base, step, here_ref, *refs):
    sums, refs = refs[:4], refs[4:]
    if top:
        square_ref, refs = refs[0], refs[1:]
    hi_ref, lo_ref, prior_ref = refs[:3]
    normal_ref, panel_ref, phi, plo = refs[-4:]
    a, r, c = here_ref[0], here_ref[1], here_ref[2]
    g, h = pl.program_id(0), pl.program_id(1)
    t = prior_ref.shape[1]
    k = base + step * g
    odd = r % 2
    part = (h + odd) % 2
    use = (part if halved else g) == a
    x = lax.broadcasted_iota(jnp.int32, (t, t), 0)
    y = lax.broadcasted_iota(jnp.int32, (t, t), 1)

    def total(index, columns):
        keep, keep_other, late, late_other = [x[index, :, columns] for x in sums]
        return jnp.where(use, keep, keep_other) + jnp.where(use, late, late_other).astype(F32)

    for i in range(q // 2):
        z = h * (q // 2) + i
        index = jnp.where(odd == 1, q // 2 - 1 - i, i)
        rows = total(index, slice(0, kc * t))
        for k2 in range(kc):
            tile = rows[:, k2 * t : (k2 + 1) * t]
            same = jnp.logical_and(k == k2, c == z * n_row + r)
            tile = tile + jnp.where(jnp.logical_and(same, x == y), prior_ref[k2 : k2 + 1, :], 0.0)
            normal_ref[pl.ds(i * t * kc + k2, t, stride=kc), :] = tile
        if top:
            first = pl.multiple_of((z * n_row + r) * t, t)
            rows = square_ref[pl.ds(first, t), :]
        else:
            rows = total(index, slice(kc * t, None))
        high = rows.astype(BF16)
        phi[i * t : (i + 1) * t, :] = high
        plo[i * t : (i + 1) * t, :] = (rows - high.astype(F32)).astype(BF16)

    def product(u, v):
        return lax.dot_general(u, v, (((1,), (1,)), ((), ())), preferred_element_type=F32)

    width = panel_ref.shape[1]
    for lo in range(0, width, WIDE):
        hi = lo + WIDE
        panel_ref[:, lo:hi] = (
            product(phi[:, :hi], hi_ref[lo:hi, :hi])
            + product(phi[:, :hi], lo_ref[lo:hi, :hi])
            + product(plo[:, :hi], hi_ref[lo:hi, :hi])
        )


def finish(outputs, here, sums, square, inverse, prior, halved, base, step, count, kc, q, n_row):
    t = prior.shape[1]
    width = inverse[0].shape[0]
    top = len(square) == 1
    arrays = [*sums, *square, *inverse, prior]

    def spec(x, mine):
        if x.ndim == 3:
            block = (q // 2,) + x.shape[1:]
            if halved:
                return pl.BlockSpec(block, lambda g, h, p: (0, 0, 0))
            def place(g, h, p):
                part = jnp.where((g == p[0]) == mine, h, 1 - p[0] if mine else p[0])
                return ((part + p[1]) % 2, 0, 0)

            return pl.BlockSpec(block, place)
        return pl.BlockSpec(x.shape, lambda g, h, p: (0, 0))

    shapes = (
        jax.ShapeDtypeStruct((kc * q * t * kc, t), F32),
        jax.ShapeDtypeStruct((kc * q * t, width), F32),
    )
    n_in = 1 + len(arrays)
    half = q // 2 * t

    def place(g, h, p):
        return (2 * (base + step * g) + h, 0)

    return pl.pallas_call(
        functools.partial(finish_kernel, top, halved, kc, q, n_row, base, step),
        grid_spec=pltpu.PrefetchScalarGridSpec(
            num_scalar_prefetch=1,
            grid=(count, 2),
            in_specs=[spec(x, i % 2 == 0) for i, x in enumerate(arrays)] + [pl.BlockSpec(memory_space=pl.ANY)] * len(outputs),
            out_specs=(pl.BlockSpec((half * kc, t), place), pl.BlockSpec((half, width), place)),
            scratch_shapes=[pltpu.VMEM((half, width), BF16)] * 2,
        ),
        out_shape=shapes,
        input_output_aliases={n_in: 0, n_in + 1: 1} if outputs else {},
        compiler_params=pltpu.CompilerParams(vmem_limit_bytes=52 * 1024 * 1024),
        cost_estimate=SHORT,
        name=f"finish_{base}",
    )(here, *arrays, *outputs)


def finish_fast(prior, leading, gathered, weights):
    packed, arrived, priors, *begun = leading
    lead_own, lead_other, main, rest = gathered
    kc, t = prior.shape
    n_row = lax.axis_size("row")
    q = lax.axis_size("col") // n_row
    m = len(main)
    a, r, c = [lax.axis_index(x) for x in ("arc", "row", "col")]
    here = jnp.stack([a, r, c]).astype(jnp.int32)
    half = q // 2

    def pair(x):
        return [x, swap(x, "arc")]

    def rows_of(keep, late):
        return pair(keep) + pair(late)

    rows = lead_own.shape[1]
    wide = lax.optimization_barrier(jnp.concatenate(weights, axis=1))
    wide_halves = [wide[:rows], wide[rows:]]
    lead_halves = [weights[0][:rows], weights[0][rows:]]

    def product(blocks, places, group, dtype, *wait):
        total = 0.0
        zero = after(jnp.int32(0), *wait)
        for x, place, w in zip(blocks, places, group):
            x = lax.dynamic_index_in_dim(x, place + zero, 0, keepdims=False)
            total += jnp.einsum("qrt,ru->qtu", x, w, preferred_element_type=F32)
        return lax.optimization_barrier(total.astype(dtype))

    def split(x):
        return x.reshape((2 * n_row, half) + x.shape[1:])

    other_owner = (r + 1) % n_row
    x = [split(lead_own), split(lead_other)]
    at = [2 * other_owner + a] * 2, [2 * r + a] * 2
    lead_sent = product(x, at[0], lead_halves, BF16, packed)
    lead_late = swap(lead_sent, "row")
    lead_keep = product(x, at[1], lead_halves, F32, lead_sent)
    main = [[by_owner(x)] for x in main]
    blocks = pair(packed) + pair(arrived)
    sent = product(main[0], [other_owner], [wide], BF16, lead_keep, blocks[3])
    late = [swap(sent, "row")]
    symmetric = assemble(*blocks, priors, sent, *begun)

    ahead = {7: late}
    for state in inverse_cholesky_steps(symmetric, ahead):
        pass
    inverse = state[2:]

    wait = product(main[0], [r], [wide], F32, state[1])
    kept = [wait]
    for i in range(1, m):
        wait = product(main[i], [other_owner], [wide], BF16, wait)
        late.append(swap(wait, "row"))
    args = (inverse, prior)
    shape = (kc, q, n_row)
    gate = after(here, wait)
    out = finish([], gate, rows_of(lead_keep, lead_late), [symmetric], *args, True, 0, 1, 1, *shape)
    out = finish(out, here, rows_of(kept[0], late[0]), [], *args, False, 1, m, 2, *shape)
    wait = out[1]
    for i in range(1, m):
        wait = product(main[i], [r], [wide], F32, wait)
        kept.append(wait)

    chunks = [(1 + i, m, 2, False) for i in range(m)]
    rest_blocks = []
    for i, x in enumerate(rest):
        received = swap(core_half(by_owner(x), after(1 - a, wait)), "arc")
        rest_blocks.append([split(x), received])
        at = [2 * other_owner + a, other_owner]
        wait = product(rest_blocks[-1], at, wide_halves, BF16, wait)
        late.append(swap(wait, "row"))
        chunks.append((1 + 2 * m + i, 1, 1, True))
    for x in rest_blocks:
        wait = product(x, [2 * r + a, r], wide_halves, F32, wait, *late[1:m])
        kept.append(wait)
    gate = after(here, wait)
    for (base, step, count, halved), keep, x in list(zip(chunks, kept, late))[1:]:
        out = finish(out, gate, rows_of(keep, x), [], *args, halved, base, step, count, *shape)
    normal, panel = out
    return (normal.reshape(kc * q, 1, t, kc, 1, t), panel.reshape(kc * q, 1, t, -1))


def body(design, obs_weight, prior):
    n_row = lax.axis_size("row")
    n_col = lax.axis_size("col")
    a = lax.axis_index("arc")
    r = lax.axis_index("row")
    c = lax.axis_index("col")
    rows, kc, _, t = design.shape
    q = n_col // n_row
    m = (kc - 1) // 2
    width = n_col * t
    first = a == 0
    fast = t == 128 and width == 4 * WIDE and n_row == 2
    order = ring_order(n_col, n_row)
    own = lax.optimization_barrier(jnp.transpose(design[:, :, 0, :], (1, 0, 2)))

    extra = jnp.concatenate([p[None] for p in split3(prior[0, 0])] + [jnp.zeros((13, t), BF16)])
    lead_in = lax.pad(design[:, 0, 0, :], BF16(0), ((0, 16, 0), (0, 0, 0)))
    lead_in = lead_in + lax.pad(extra, BF16(0), ((rows, 0, 0), (0, 0, 0)))
    lead_all = gather_cols(lead_in, order)
    other = swap(own, "arc")
    weight_other = swap(obs_weight, "arc")
    both = jnp.concatenate([own, other], axis=1)
    w2 = jnp.concatenate([obs_weight, weight_other])
    weighted = jnp.transpose(weigh(both, w2), (1, 0, 2)).reshape(2 * rows, kc * t)
    weighted = lax.optimization_barrier(weighted)

    def share(i, *wait):
        return lax.dynamic_index_in_dim(both, after(1 + m * a + i, *wait), 0, keepdims=False)

    first_share = share(0)
    main = [gather_cols(first_share, order)]
    zero = after(jnp.int32(0), first_share, weighted)
    lead_own = lax.dynamic_slice_in_dim(lead_all, zero, rows, 1)
    lead_own = lax.optimization_barrier(lead_own)
    lead_other = swap(lead_own, "arc")
    shares = [share(i, lead_own) for i in range(1, m)]
    main += [gather_cols(x, order) for x in shares]
    priors = lax.dynamic_slice_in_dim(lead_all, rows + zero, 3, 1)
    priors = jnp.sum(priors.astype(F32), axis=1)
    priors = jnp.concatenate([priors[order.index(x)] for x in range(n_col)])

    if fast:
        lead_weighted, packed = lead_blocks(
            lead_own, lead_other, w2, order, rows
        )
        arrived = swap(packed, "row")
        first_use = packed
    else:
        flat = jnp.concatenate([lead_own, lead_other], axis=1)
        flat = jnp.stack([flat[order.index(x)] for x in range(n_col)])
        lead_weighted = jnp.transpose(weigh(flat, w2), (1, 0, 2)).reshape(2 * rows, width)
        first_use = lead_weighted
        half = n_col // 2
        square = jnp.einsum(
            "crt,ru->ctu",
            lax.dynamic_slice_in_dim(flat, half * a, half, 0),
            lead_weighted,
            preferred_element_type=F32,
        )
        square = lax.psum(square, "row")
        square_other = swap(square, "arc")
        square = jnp.concatenate(
            [jnp.where(first, square, square_other), jnp.where(first, square_other, square)]
        ).reshape(width, width)
        symmetric = 0.5 * (square + square.T) + jnp.diag(priors)
    rest_in = [
        lax.dynamic_slice(both, (after(i, first_use, *shares), 0, 0), (1, rows, t))[0]
        for i in range(1 + 2 * m, kc)
    ]
    rest = [gather_cols(x, order) for x in rest_in]

    split = (weighted[:rows], weighted[rows:])
    lead_split = (lead_weighted[:rows], lead_weighted[rows:])

    if fast:
        return finish_fast(
            prior.reshape(kc, t),
            (packed, arrived, priors, *rest_in),
            (lead_own, lead_other, main, rest),
            (weighted, lead_weighted),
        )

    halves = [core_half(by_owner(x), a) for x in (lead_own, lead_other)]
    n_lead = partial_sums(halves, split)
    main_sums = [partial_sums([by_owner(x)], [weighted], [lead_weighted]) for x in main]
    rest_sums = [partial_sums(core_halves(by_owner(x)), split, lead_split) for x in rest]
    *_, (_, inverse, _, _) = inverse_cholesky_steps(symmetric, {})

    def sides(x):
        y = swap(x, "arc")
        return jnp.where(first, x, y), jnp.where(first, y, x)

    n_rows, p_rows = [None] * kc, [None] * kc
    n_rows[0] = jnp.concatenate(sides(n_lead[0]))
    for i, (n, p) in enumerate(main_sums):
        n_rows[1 + i], n_rows[1 + m + i] = sides(n)
        p_rows[1 + i], p_rows[1 + m + i] = sides(p)
    for i, (n, p) in enumerate(rest_sums):
        n_rows[1 + 2 * m + i] = jnp.concatenate(sides(n))
        p_rows[1 + 2 * m + i] = jnp.concatenate(sides(p))

    def in_order(x):
        x = jnp.stack(x)
        return jnp.where(r % 2 == 1, x[:, ::-1], x)

    tiles = in_order(n_rows).reshape(kc * q, t, kc, t)
    tile_rows = jnp.arange(kc * q, dtype=jnp.int32) * n_row + r
    tile_cols = jnp.arange(kc, dtype=jnp.int32) * n_col + c
    same = (tile_rows[:, None] == tile_cols[None, :]).astype(F32)
    identity = jnp.eye(t, dtype=F32)
    added = same[:, None, :, None] * identity[None, :, None, :] * prior.reshape(kc, t)[None, None]
    normal = (tiles + added).reshape(kc * q, 1, t, kc, 1, t)
    top = lax.dynamic_index_in_dim(symmetric.reshape(q, n_row, t, width), r, 1, keepdims=False)
    panel_rows = jnp.concatenate([top[None], in_order(p_rows[1:])])
    result = jnp.einsum(
        "rk,jk->rj",
        panel_rows.reshape(kc * q * t, width),
        inverse,
        precision=lax.Precision.HIGH,
        preferred_element_type=F32,
    )
    return (normal, result.reshape(kc * q, 1, t, width))


def solution(mesh):
    placed = (P(("arc", "row"), None, "col", None), P(("arc", "row")), P(None, "col", None))
    return jax.shard_map(
        body,
        mesh=mesh,
        in_specs=placed,
        out_specs=(P(None, "row", None, None, "col", None), P(None, "row", None, None)),
        check_vma=False,
    )
```

```python
import functools

import jax
import jax.numpy as jnp
from jax import lax
from jax.experimental import pallas as pl
from jax.experimental.pallas import tpu as pltpu
from jax.sharding import PartitionSpec as P

F32 = jnp.float32
BF16 = jnp.bfloat16

SHORT = pl.CostEstimate(flops=10**6, bytes_accessed=10**5, transcendentals=0)
BLOCK = 128
STRIP = 16


def dot_tn(x, y):
    return lax.dot_general(
        x, y, (((0,), (0,)), ((), ())), precision=lax.Precision.HIGHEST, preferred_element_type=F32
    )


def dot_nn(x, y):
    return jnp.dot(x, y, precision=lax.Precision.HIGHEST, preferred_element_type=F32)


def inverse_factor(square):
    n = square.shape[0]
    count = n // STRIP
    row_id = lax.broadcasted_iota(jnp.int32, (STRIP, n), 0)
    left = [square[i * STRIP : (i + 1) * STRIP, :] for i in range(count)]
    lane = lax.broadcasted_iota(jnp.int32, (STRIP, n), 1)
    right = [(lane == row_id + i * STRIP).astype(F32) for i in range(count)]
    done = []
    for b in range(count):
        ps, pe = left[b], right[b]
        columns = [
            jnp.broadcast_to(ps[:, b * STRIP + l : b * STRIP + l + 1], (STRIP, n))
            for l in range(STRIP)
        ]
        scale = jnp.zeros((STRIP, n), F32)
        for j in range(STRIP):
            rs = lax.rsqrt(columns[j][j : j + 1, :])
            col = columns[j] * rs
            below = jnp.where(row_id > j, col, 0.0)
            ps = ps - below * (ps[j : j + 1, :] * rs)
            pe = pe - below * (pe[j : j + 1, :] * rs)
            for l in range(j + 1, STRIP):
                columns[l] = columns[l] - col * (columns[l][j : j + 1, :] * rs)
            scale = jnp.where(row_id == j, rs, scale)
        ps = ps * scale
        pe = pe * scale
        done.append(pe)
        if b + 1 < count:
            update = dot_tn(ps, jnp.concatenate([ps, pe], axis=1))
            for i in range(b + 1, count):
                left[i] = left[i] - update[i * STRIP : (i + 1) * STRIP, :n]
                right[i] = right[i] - update[i * STRIP : (i + 1) * STRIP, n:]
    return jnp.concatenate(done, axis=0)


def factor_step(k, blocks, s_ref, *refs):
    lo, hi = k * BLOCK, (k + 1) * BLOCK
    u_out, e_out = refs[-2:]
    if k:
        u_ref, e_ref = refs[:2]
        above = u_ref[:, lo:hi]
        diag = s_ref[:, lo:hi] - dot_tn(above, above)
    else:
        diag = s_ref[:, lo:hi]
    inverse = inverse_factor(diag)
    width = blocks * BLOCK
    u_out[:, :hi] = jnp.zeros((BLOCK, hi), F32)
    if k + 1 < blocks:
        rest = s_ref[:, hi:]
        if k:
            rest = rest - dot_tn(above, u_ref[:, hi:])
        u_out[:, hi:] = dot_nn(inverse, rest)
        e_out[:, hi:] = jnp.zeros((BLOCK, width - hi), F32)
    if k:
        e_out[:, :lo] = -dot_nn(inverse, dot_tn(above, e_ref[:, :lo]))
    e_out[:, lo:hi] = inverse


def inverse_cholesky_steps(square, ahead):
    width = square.shape[0]
    blocks = width // BLOCK
    shape = jax.ShapeDtypeStruct((width, width), F32)
    state = None
    for k in range(blocks):
        gates = []
        if k in ahead:
            gate = after(jnp.zeros((1,), jnp.int32), *ahead[k])
            gates = [gate]
        row = pl.BlockSpec((BLOCK, width), lambda i, k=k: (k, 0))
        seen = pl.BlockSpec((k * BLOCK, width), lambda i: (0, 0))
        state = pl.pallas_call(
            functools.partial(factor_step, k, blocks),
            grid=(1,),
            out_shape=(shape, shape),
            in_specs=[row]
            + ([seen, seen] if k else [])
            + [pl.BlockSpec(memory_space=pltpu.SMEM)] * len(gates),
            out_specs=(row, row),
            input_output_aliases={1: 0, 2: 1} if k else {},
            compiler_params=pltpu.CompilerParams(vmem_limit_bytes=40 * 1024 * 1024),
            cost_estimate=SHORT,
            name=f"factor_{k}",
        )(square, *(state or ()), *gates)
        yield state


def ring_order(n, owners):
    order = []
    for owner in range(owners):
        order += list(range(owner, n, owners))[:: -1 if owner % 2 else 1]
    return order


def swap(x, axis, shift=1):
    n = lax.axis_size(axis)
    return lax.ppermute(x, axis, [(i, (i + shift) % n) for i in range(n)])


def after(index, *others):
    for x in others:
        one = lax.slice(x, (0,) * x.ndim, (1,) * x.ndim).reshape(()).astype(F32)
        index = index + jnp.minimum(jnp.abs(one), 0.0).astype(jnp.int32)
    return index


def gather_cols(x, order):
    return lax.all_gather(x, "col", axis=0, tiled=False, axis_index_groups=[order])


def weigh(x, w):
    return (x.astype(F32) * w[:, None]).astype(BF16)


def split3(x):
    hi = lax.reduce_precision(x, 8, 7)
    mid = lax.reduce_precision(x - hi, 8, 7)
    return [y.astype(BF16) for y in (hi, mid, x - hi - mid)]


def by_owner(x):
    n_row = lax.axis_size("row")
    return x.reshape((n_row, x.shape[0] // n_row) + x.shape[1:])


def product_of(blocks, owner, group):
    total = 0.0
    for x, w in zip(blocks, group):
        mine = lax.dynamic_index_in_dim(x, owner, 0, keepdims=False)
        total += jnp.einsum("qrt,ru->qtu", mine, w, preferred_element_type=F32)
    return total


def sends(blocks, groups, *wait):
    n_row = lax.axis_size("row")
    r = after(lax.axis_index("row"), *wait)
    parts = [
        [product_of(blocks, (r + d) % n_row, w).astype(BF16) for d in range(1, n_row)]
        for w in groups
    ]
    return lax.optimization_barrier(parts)


def keeps(blocks, groups, *wait):
    r = after(lax.axis_index("row"), *wait)
    return lax.optimization_barrier([product_of(blocks, r, w) for w in groups])


def receive(sent):
    return [[swap(x, "row", 1 + i) for i, x in enumerate(parts)] for parts in sent]


def partial_sums(blocks, *groups):
    totals = []
    for total, parts in zip(keeps(blocks, groups), receive(sends(blocks, groups))):
        for x in parts:
            total = total + x.astype(F32)
        totals.append(total)
    return totals


def core_half(x, core):
    half = x.shape[1] // 2
    return lax.dynamic_slice_in_dim(x, half * core, half, 1)


def core_halves(x):
    a = lax.axis_index("arc")
    return [core_half(x, a), swap(core_half(x, 1 - a), "arc")]


PAIRS = (((0, 0), (0, 1), (0, 2), (0, 3), (3, 3)), ((1, 1), (1, 2), (1, 3), (2, 2), (2, 3)))
WIDE = 256


def lead_kernel(order, rows, pairs_ref, own_ref, other_ref, w_ref, weighted_ref, s_ref, flat_ref):
    @pl.when(pl.program_id(0) == 0)
    def _():
        t = own_ref.shape[2]
        for pos, c in enumerate(order):
            for arc, ref in enumerate((own_ref, other_ref)):
                x = ref[pos, :rows, :]
                place = (pl.ds(arc * rows, rows), pl.ds(c * t, t))
                flat_ref[place] = x
                weighted_ref[place] = (x.astype(F32) * w_ref[pl.ds(arc * rows, rows), :]).astype(BF16)

    def columns(entry):
        return pl.ds(pl.multiple_of(pairs_ref[2 * pl.program_id(0) + entry] * WIDE, WIDE), WIDE)

    def product(x, y):
        return lax.dot_general(x, y, (((0,), (0,)), ((), ())), preferred_element_type=F32)

    i, j = columns(0), columns(1)
    s_ref[0] = 0.5 * (
        product(flat_ref[:, i], weighted_ref[:, j]) + product(weighted_ref[:, i], flat_ref[:, j])
    )


def lead_blocks(own, other, weight_columns, order, rows):
    n, padded, t = own.shape
    width = n * t
    count = len(PAIRS[0])
    pairs = jnp.array(PAIRS, jnp.int32).reshape(2, 2 * count)[lax.axis_index("arc")]
    whole = pl.BlockSpec((n, padded, t), lambda s, p: (0, 0, 0))
    return pl.pallas_call(
        functools.partial(lead_kernel, order, rows),
        grid_spec=pltpu.PrefetchScalarGridSpec(
            num_scalar_prefetch=1,
            grid=(count,),
            in_specs=[whole, whole, pl.BlockSpec((2 * rows, t), lambda s, p: (0, 0))],
            out_specs=(
                pl.BlockSpec((2 * rows, width), lambda s, p: (0, 0)),
                pl.BlockSpec((1, WIDE, WIDE), lambda s, p: (s, 0, 0)),
            ),
            scratch_shapes=[pltpu.VMEM((2 * rows, width), BF16)],
        ),
        out_shape=(
            jax.ShapeDtypeStruct((2 * rows, width), BF16),
            jax.ShapeDtypeStruct((count, WIDE, WIDE), F32),
        ),
        compiler_params=pltpu.CompilerParams(vmem_limit_bytes=52 * 1024 * 1024),
        cost_estimate=SHORT,
        name="lead_blocks",
    )(pairs, own, other, weight_columns)


def assemble_kernel(table_ref, mine_ref, theirs_ref, late_ref, late_other_ref, prior_ref, out_ref):
    i, j = pl.program_id(0), pl.program_id(1)
    entry = table_ref[4 * i + j]
    at = entry % 8
    block = jnp.where(entry < 8, mine_ref[at] + late_ref[at], theirs_ref[at] + late_other_ref[at])

    @pl.when(i < j)
    def _():
        out_ref[...] = block

    @pl.when(i > j)
    def _():
        out_ref[...] = block.T

    @pl.when(i == j)
    def _():
        x = lax.broadcasted_iota(jnp.int32, block.shape, 0)
        y = lax.broadcasted_iota(jnp.int32, block.shape, 1)
        out_ref[...] = block + jnp.where(x == y, prior_ref[...], 0.0)


def assemble(mine, theirs, late, late_other, priors, *wait):
    width = priors.shape[0]
    tables = [[0] * 16, [0] * 16]
    for core in range(2):
        for slot, (i, j) in enumerate(PAIRS[core]):
            for a in range(2):
                tables[a][4 * i + j] = tables[a][4 * j + i] = slot + (0 if a == core else 8)
    table = after(jnp.array(tables, jnp.int32)[lax.axis_index("arc")], *wait)
    blocks = pl.BlockSpec(mine.shape, lambda i, j, p: (0, 0, 0))
    return pl.pallas_call(
        assemble_kernel,
        grid_spec=pltpu.PrefetchScalarGridSpec(
            num_scalar_prefetch=1,
            grid=(4, 4),
            in_specs=[blocks] * 4 + [pl.BlockSpec((1, WIDE), lambda i, j, p: (0, j))],
            out_specs=pl.BlockSpec((WIDE, WIDE), lambda i, j, p: (i, j)),
        ),
        out_shape=jax.ShapeDtypeStruct((width, width), F32),
        compiler_params=pltpu.CompilerParams(vmem_limit_bytes=24 * 1024 * 1024),
        cost_estimate=SHORT,
        name="assemble",
    )(table, mine, theirs, late, late_other, priors[None])


def finish_kernel(top, halved, kc, q, n_row, base, step, here_ref, *refs):
    sums, refs = refs[:4], refs[4:]
    if top:
        square_ref, refs = refs[0], refs[1:]
    hi_ref, lo_ref, prior_ref = refs[:3]
    normal_ref, panel_ref, parts = refs[-3:]
    a, r, c = here_ref[0], here_ref[1], here_ref[2]
    g = pl.program_id(0)
    t = prior_ref.shape[1]
    k = base + step * g
    odd = r % 2
    size = q * t
    x = lax.broadcasted_iota(jnp.int32, (t, t), 0)
    y = lax.broadcasted_iota(jnp.int32, (t, t), 1)

    for z in range(q):
        at = jnp.where(odd == 1, q - 1 - z, z)
        core, index = (at // (q // 2), at % (q // 2)) if halved else (g, at)
        use = core == a

        def total(columns):
            keep, keep_other, late, late_other = [ref[index, :, columns] for ref in sums]
            return jnp.where(use, keep, keep_other) + jnp.where(use, late, late_other).astype(F32)

        rows = total(slice(0, kc * t))
        for k2 in range(kc):
            tile = rows[:, k2 * t : (k2 + 1) * t]
            same = jnp.logical_and(k == k2, c == z * n_row + r)
            tile = tile + jnp.where(jnp.logical_and(same, x == y), prior_ref[k2 : k2 + 1, :], 0.0)
            normal_ref[pl.ds(z * t * kc + k2, t, stride=kc), :] = tile
        if top:
            first = pl.multiple_of((z * n_row + r) * t, t)
            rows = square_ref[pl.ds(first, t), :]
        else:
            rows = total(slice(kc * t, None))
        high = rows.astype(BF16)
        parts[z * t : (z + 1) * t, :] = high
        parts[size + z * t : size + (z + 1) * t, :] = (rows - high.astype(F32)).astype(BF16)

    def product(u, v):
        return lax.dot_general(u, v, (((1,), (1,)), ((), ())), preferred_element_type=F32)

    width = panel_ref.shape[1]
    for lo in range(0, width, WIDE):
        hi = lo + WIDE
        both = product(parts[:, :hi], hi_ref[lo:hi, :hi])
        panel_ref[:, lo:hi] = (
            both[:size] + both[size:] + product(parts[:size, :hi], lo_ref[lo:hi, :hi])
        )


def finish(outputs, here, sums, square, inverse, prior, halved, base, step, count, kc, q, n_row):
    t = prior.shape[1]
    width = inverse[0].shape[0]
    top = len(square) == 1
    arrays = [*sums, *square, *inverse, prior]

    def spec(x):
        if x.ndim == 3:
            return pl.BlockSpec(x.shape, lambda g, p: (0, 0, 0))
        return pl.BlockSpec(x.shape, lambda g, p: (0, 0))

    shapes = (
        jax.ShapeDtypeStruct((kc * q * t * kc, t), F32),
        jax.ShapeDtypeStruct((kc * q * t, width), F32),
    )
    n_in = 1 + len(arrays)

    def place(g, p):
        return (base + step * g, 0)

    return pl.pallas_call(
        functools.partial(finish_kernel, top, halved, kc, q, n_row, base, step),
        grid_spec=pltpu.PrefetchScalarGridSpec(
            num_scalar_prefetch=1,
            grid=(count,),
            in_specs=[spec(x) for x in arrays] + [pl.BlockSpec(memory_space=pl.ANY)] * len(outputs),
            out_specs=(pl.BlockSpec((q * t * kc, t), place), pl.BlockSpec((q * t, width), place)),
            scratch_shapes=[pltpu.VMEM((2 * q * t, width), BF16)],
        ),
        out_shape=shapes,
        input_output_aliases={n_in: 0, n_in + 1: 1} if outputs else {},
        compiler_params=pltpu.CompilerParams(vmem_limit_bytes=52 * 1024 * 1024),
        cost_estimate=SHORT,
        name=f"finish_{base}",
    )(here, *arrays, *outputs)


def finish_fast(prior, leading, gathered, weights):
    packed, arrived, priors = leading
    lead_own, lead_other, main, rest = gathered
    kc, t = prior.shape
    n_row = lax.axis_size("row")
    q = lax.axis_size("col") // n_row
    m = len(main)
    a, r, c = [lax.axis_index(x) for x in ("arc", "row", "col")]
    here = jnp.stack([a, r, c]).astype(jnp.int32)
    half = q // 2

    def pair(x):
        return [x, swap(x, "arc")]

    def rows_of(keep, late):
        return pair(keep) + pair(late)

    wide = lax.optimization_barrier(jnp.concatenate(weights, axis=1))
    rows = wide.shape[0] // 2
    other_owner = (r + 1) % n_row

    def product(blocks, place, w, dtype, *wait):
        x = lax.dynamic_index_in_dim(blocks, after(place, *wait), 0, keepdims=False)
        total = jnp.einsum("qrt,ru->qtu", x, w, preferred_element_type=F32)
        return lax.optimization_barrier(total.astype(dtype))

    def half_products(own, other, w, *wait):
        mine = core_half(by_owner(own), after(a, *wait))
        x = jnp.concatenate([mine[:, :, :rows], other[:, :, :rows]], axis=2)
        total = jnp.einsum("oqrt,ru->oqtu", x, w, preferred_element_type=F32)
        total = lax.optimization_barrier(total)
        send = lax.dynamic_index_in_dim(total, other_owner, 0, keepdims=False).astype(BF16)
        return send, lax.dynamic_index_in_dim(total, r, 0, keepdims=False)

    x = core_half(by_owner(lead_other), a)
    lead_sent, lead_keep = half_products(lead_own, x, wide[:, : kc * t], packed)
    lead_late = swap(lead_sent, "row")
    main = [by_owner(x) for x in main]
    blocks = pair(packed) + pair(arrived)
    sent = product(main[0], other_owner, wide, BF16, lead_keep, lead_late, blocks[3])
    late = [swap(sent, "row")]
    symmetric = assemble(*blocks, priors, sent)

    ahead = {7: late}
    for state in inverse_cholesky_steps(symmetric, ahead):
        pass
    high = lax.reduce_precision(state[1], 8, 7)
    inverse = (high.astype(BF16), (state[1] - high).astype(BF16))
    inverse = lax.optimization_barrier(inverse)

    wait = inverse[1]
    begun = []
    for i in range(1, m):
        wait = product(main[i], other_owner, wide, BF16, wait)
        pieces = [swap(wait[:half], "row"), swap(wait[half:], "row")]
        begun.append(pieces)
        late.append(jnp.concatenate(pieces))
    kept = [product(main[0], r, wide, F32, wait)]
    args = (inverse, prior)
    shape = (kc, q, n_row)
    gate = after(here, kept[0])
    out = finish([], gate, rows_of(lead_keep, lead_late), [symmetric], *args, True, 0, 1, 1, *shape)
    wait = out[1]
    rest_kept = []
    for x in rest:
        received = swap(core_half(by_owner(x), after(1 - a, wait, *[x[0] for x in begun])), "arc")
        sent, keep = half_products(x, received, wide, wait)
        late.append(swap(sent, "row"))
        rest_kept.append(keep)
        wait = sent
    gate = after(here, wait, *[x[1] for x in begun])
    out = finish(out, gate, rows_of(kept[0], late[0]), [], *args, False, 1, m, 2, *shape)
    wait = out[1]
    for i in range(1, m):
        wait = product(main[i], r, wide, F32, wait)
        kept.append(wait)
    kept += rest_kept
    chunks = [(1 + i, m, 2, False) for i in range(m)]
    chunks += [(1 + 2 * m + i, 1, 1, True) for i in range(len(rest))]
    gate = after(here, wait)
    for (base, step, count, halved), keep, x in list(zip(chunks, kept, late))[1:]:
        out = finish(out, gate, rows_of(keep, x), [], *args, halved, base, step, count, *shape)
    normal, panel = out
    return (normal.reshape(kc * q, 1, t, kc, 1, t), panel.reshape(kc * q, 1, t, -1))


def body(design, obs_weight, prior):
    n_row = lax.axis_size("row")
    n_col = lax.axis_size("col")
    a = lax.axis_index("arc")
    r = lax.axis_index("row")
    c = lax.axis_index("col")
    rows, kc, _, t = design.shape
    q = n_col // n_row
    m = (kc - 1) // 2
    width = n_col * t
    first = a == 0
    fast = t == 128 and width == 4 * WIDE and n_row == 2
    order = ring_order(n_col, n_row)
    own = lax.optimization_barrier(jnp.transpose(design[:, :, 0, :], (1, 0, 2)))

    extra = jnp.concatenate([p[None] for p in split3(prior[0, 0])] + [jnp.zeros((13, t), BF16)])
    lead_in = lax.pad(design[:, 0, 0, :], BF16(0), ((0, 16, 0), (0, 0, 0)))
    lead_in = lead_in + lax.pad(extra, BF16(0), ((rows, 0, 0), (0, 0, 0)))
    lead_all = gather_cols(lead_in, order)
    other = swap(own, "arc")
    weight_other = swap(obs_weight, "arc")
    both = jnp.concatenate([own, other], axis=1)
    w2 = jnp.concatenate([obs_weight, weight_other])
    weighted = jnp.transpose(weigh(both, w2), (1, 0, 2)).reshape(2 * rows, kc * t)
    weighted = lax.optimization_barrier(weighted)

    def hold(x, *others):
        return lax.optimization_barrier((x, others))[0]

    shares = [lax.dynamic_index_in_dim(both, 1 + m * a + i, 0, keepdims=False) for i in range(m)]
    shares = list(lax.optimization_barrier(tuple(shares)))
    weight_columns = jnp.broadcast_to(w2[:, None], (2 * rows, t))
    main = [gather_cols(shares[0], order)]
    lead_own = hold(lead_all, shares, weighted, weight_columns)
    shares = [hold(x, lead_own) for x in shares[1:]]
    main += [gather_cols(x, order) for x in shares]
    lead_other = swap(lead_own, "arc")
    priors = jnp.sum(lead_own[:, rows : rows + 3].astype(F32), axis=1)
    priors = jnp.concatenate([priors[order.index(x)] for x in range(n_col)])

    if fast:
        lead_weighted, packed = lead_blocks(
            lead_own, lead_other, weight_columns, order, rows
        )
        arrived = swap(packed, "row")
        first_use = packed
    else:
        flat = jnp.concatenate([lead_own[:, :rows], lead_other[:, :rows]], axis=1)
        flat = jnp.stack([flat[order.index(x)] for x in range(n_col)])
        lead_weighted = jnp.transpose(weigh(flat, w2), (1, 0, 2)).reshape(2 * rows, width)
        first_use = lead_weighted
        half = n_col // 2
        square = jnp.einsum(
            "crt,ru->ctu",
            lax.dynamic_slice_in_dim(flat, half * a, half, 0),
            lead_weighted,
            preferred_element_type=F32,
        )
        square = lax.psum(square, "row")
        square_other = swap(square, "arc")
        square = jnp.concatenate(
            [jnp.where(first, square, square_other), jnp.where(first, square_other, square)]
        ).reshape(width, width)
        symmetric = 0.5 * (square + square.T) + jnp.diag(priors)
    rest = [gather_cols(hold(x, first_use, shares), order) for x in own[1 + 2 * m :]]

    if fast:
        return finish_fast(
            prior.reshape(kc, t),
            (packed, arrived, priors),
            (lead_own, lead_other, main, rest),
            (weighted, lead_weighted),
        )

    halves = [core_half(by_owner(x[:, :rows]), a) for x in (lead_own, lead_other)]
    split = (weighted[:rows], weighted[rows:])
    lead_split = (lead_weighted[:rows], lead_weighted[rows:])
    n_lead = partial_sums(halves, split)
    main_sums = [partial_sums([by_owner(x)], [weighted], [lead_weighted]) for x in main]
    rest_sums = [partial_sums(core_halves(by_owner(x)), split, lead_split) for x in rest]
    *_, (_, inverse) = inverse_cholesky_steps(symmetric, {})

    def sides(x):
        y = swap(x, "arc")
        return jnp.where(first, x, y), jnp.where(first, y, x)

    n_rows, p_rows = [None] * kc, [None] * kc
    n_rows[0] = jnp.concatenate(sides(n_lead[0]))
    for i, (n, p) in enumerate(main_sums):
        n_rows[1 + i], n_rows[1 + m + i] = sides(n)
        p_rows[1 + i], p_rows[1 + m + i] = sides(p)
    for i, (n, p) in enumerate(rest_sums):
        n_rows[1 + 2 * m + i] = jnp.concatenate(sides(n))
        p_rows[1 + 2 * m + i] = jnp.concatenate(sides(p))

    def in_order(x):
        x = jnp.stack(x)
        return jnp.where(r % 2 == 1, x[:, ::-1], x)

    tiles = in_order(n_rows).reshape(kc * q, t, kc, t)
    tile_rows = jnp.arange(kc * q, dtype=jnp.int32) * n_row + r
    tile_cols = jnp.arange(kc, dtype=jnp.int32) * n_col + c
    same = (tile_rows[:, None] == tile_cols[None, :]).astype(F32)
    identity = jnp.eye(t, dtype=F32)
    added = same[:, None, :, None] * identity[None, :, None, :] * prior.reshape(kc, t)[None, None]
    normal = (tiles + added).reshape(kc * q, 1, t, kc, 1, t)
    top = lax.dynamic_index_in_dim(symmetric.reshape(q, n_row, t, width), r, 1, keepdims=False)
    panel_rows = jnp.concatenate([top[None], in_order(p_rows[1:])])
    result = jnp.einsum(
        "rk,jk->rj",
        panel_rows.reshape(kc * q * t, width),
        inverse,
        precision=lax.Precision.HIGH,
        preferred_element_type=F32,
    )
    return (normal, result.reshape(kc * q, 1, t, width))


def solution(mesh):
    placed = (P(("arc", "row"), None, "col", None), P(("arc", "row")), P(None, "col", None))
    return jax.shard_map(
        body,
        mesh=mesh,
        in_specs=placed,
        out_specs=(P(None, "row", None, None, "col", None), P(None, "row", None, None)),
        check_vma=False,
    )
```

```python
import functools

import jax
import jax.numpy as jnp
from jax import lax
from jax.experimental import pallas as pl
from jax.experimental.pallas import tpu as pltpu
from jax.sharding import PartitionSpec as P

F32 = jnp.float32
BF16 = jnp.bfloat16

SHORT = pl.CostEstimate(flops=10**6, bytes_accessed=10**5, transcendentals=0)
BLOCK = 128
STRIP = 16


def dot_tn(x, y):
    return lax.dot_general(
        x, y, (((0,), (0,)), ((), ())), precision=lax.Precision.HIGHEST, preferred_element_type=F32
    )


def dot_nn(x, y):
    return jnp.dot(x, y, precision=lax.Precision.HIGHEST, preferred_element_type=F32)


def inverse_factor(square):
    n = square.shape[0]
    count = n // STRIP
    row_id = lax.broadcasted_iota(jnp.int32, (STRIP, n), 0)
    left = [square[i * STRIP : (i + 1) * STRIP, :] for i in range(count)]
    lane = lax.broadcasted_iota(jnp.int32, (STRIP, n), 1)
    right = [(lane == row_id + i * STRIP).astype(F32) for i in range(count)]
    done = []
    for b in range(count):
        ps, pe = left[b], right[b]
        columns = [
            jnp.broadcast_to(ps[:, b * STRIP + l : b * STRIP + l + 1], (STRIP, n))
            for l in range(STRIP)
        ]
        scale = jnp.zeros((STRIP, n), F32)
        for j in range(STRIP):
            rs = lax.rsqrt(columns[j][j : j + 1, :])
            col = columns[j] * rs
            below = jnp.where(row_id > j, col, 0.0)
            ps = ps - below * (ps[j : j + 1, :] * rs)
            pe = pe - below * (pe[j : j + 1, :] * rs)
            for l in range(j + 1, STRIP):
                columns[l] = columns[l] - col * (columns[l][j : j + 1, :] * rs)
            scale = jnp.where(row_id == j, rs, scale)
        ps = ps * scale
        pe = pe * scale
        done.append(pe)
        if b + 1 < count:
            update = dot_tn(ps, jnp.concatenate([ps, pe], axis=1))
            for i in range(b + 1, count):
                left[i] = left[i] - update[i * STRIP : (i + 1) * STRIP, :n]
                right[i] = right[i] - update[i * STRIP : (i + 1) * STRIP, n:]
    return jnp.concatenate(done, axis=0)


def factor_step(k, blocks, s_ref, *refs):
    lo, hi = k * BLOCK, (k + 1) * BLOCK
    u_out, e_out = refs[-2:]
    if k:
        u_ref, e_ref = refs[:2]
        above = u_ref[:, lo:hi]
        diag = s_ref[:, lo:hi] - dot_tn(above, above)
    else:
        diag = s_ref[:, lo:hi]
    inverse = inverse_factor(diag)
    width = blocks * BLOCK
    u_out[:, :hi] = jnp.zeros((BLOCK, hi), F32)
    if k + 1 < blocks:
        rest = s_ref[:, hi:]
        if k:
            rest = rest - dot_tn(above, u_ref[:, hi:])
        u_out[:, hi:] = dot_nn(inverse, rest)
        e_out[:, hi:] = jnp.zeros((BLOCK, width - hi), F32)
    if k:
        e_out[:, :lo] = -dot_nn(inverse, dot_tn(above, e_ref[:, :lo]))
    e_out[:, lo:hi] = inverse


def inverse_cholesky_steps(square, ahead):
    width = square.shape[0]
    blocks = width // BLOCK
    shape = jax.ShapeDtypeStruct((width, width), F32)
    state = None
    for k in range(blocks):
        gates = []
        if k in ahead:
            gate = after(jnp.zeros((1,), jnp.int32), *ahead[k])
            gates = [gate]
        row = pl.BlockSpec((BLOCK, width), lambda i, k=k: (k, 0))
        seen = pl.BlockSpec((k * BLOCK, width), lambda i: (0, 0))
        state = pl.pallas_call(
            functools.partial(factor_step, k, blocks),
            grid=(1,),
            out_shape=(shape, shape),
            in_specs=[row]
            + ([seen, seen] if k else [])
            + [pl.BlockSpec(memory_space=pltpu.SMEM)] * len(gates),
            out_specs=(row, row),
            input_output_aliases={1: 0, 2: 1} if k else {},
            compiler_params=pltpu.CompilerParams(vmem_limit_bytes=24 * 1024 * 1024),
            cost_estimate=SHORT,
            name=f"factor_{k}",
        )(square, *(state or ()), *gates)
        yield state


def ring_order(n, owners):
    order = []
    for owner in range(owners):
        order += list(range(owner, n, owners))[:: -1 if owner % 2 else 1]
    return order


def swap(x, axis, shift=1):
    n = lax.axis_size(axis)
    return lax.ppermute(x, axis, [(i, (i + shift) % n) for i in range(n)])


def after(index, *others):
    for x in others:
        one = lax.slice(x, (0,) * x.ndim, (1,) * x.ndim).reshape(()).astype(F32)
        index = index + jnp.minimum(jnp.abs(one), 0.0).astype(jnp.int32)
    return index


def gather_cols(x, order):
    return lax.all_gather(x, "col", axis=0, tiled=False, axis_index_groups=[order])


def weigh(x, w):
    return (x.astype(F32) * w[:, None]).astype(BF16)


def split3(x):
    hi = lax.reduce_precision(x, 8, 7)
    mid = lax.reduce_precision(x - hi, 8, 7)
    return [y.astype(BF16) for y in (hi, mid, x - hi - mid)]


def by_owner(x):
    n_row = lax.axis_size("row")
    return x.reshape((n_row, x.shape[0] // n_row) + x.shape[1:])


def product_of(blocks, owner, group):
    total = 0.0
    for x, w in zip(blocks, group):
        mine = lax.dynamic_index_in_dim(x, owner, 0, keepdims=False)
        total += jnp.einsum("qrt,ru->qtu", mine, w, preferred_element_type=F32)
    return total


def sends(blocks, groups, *wait):
    n_row = lax.axis_size("row")
    r = after(lax.axis_index("row"), *wait)
    parts = [
        [product_of(blocks, (r + d) % n_row, w).astype(BF16) for d in range(1, n_row)]
        for w in groups
    ]
    return lax.optimization_barrier(parts)


def keeps(blocks, groups, *wait):
    r = after(lax.axis_index("row"), *wait)
    return lax.optimization_barrier([product_of(blocks, r, w) for w in groups])


def receive(sent):
    return [[swap(x, "row", 1 + i) for i, x in enumerate(parts)] for parts in sent]


def partial_sums(blocks, *groups):
    totals = []
    for total, parts in zip(keeps(blocks, groups), receive(sends(blocks, groups))):
        for x in parts:
            total = total + x.astype(F32)
        totals.append(total)
    return totals


def core_half(x, core):
    half = x.shape[1] // 2
    return lax.dynamic_slice_in_dim(x, half * core, half, 1)


def core_halves(x):
    a = lax.axis_index("arc")
    return [core_half(x, a), swap(core_half(x, 1 - a), "arc")]


PAIRS = (((0, 0), (0, 1), (0, 2), (0, 3), (3, 3)), ((1, 1), (1, 2), (1, 3), (2, 2), (2, 3)))
WIDE = 256


def lead_kernel(order, rows, pairs_ref, own_ref, other_ref, w_ref, weighted_ref, s_ref, flat_ref):
    @pl.when(pl.program_id(0) == 0)
    def _():
        t = own_ref.shape[2]
        for pos, c in enumerate(order):
            for arc, ref in enumerate((own_ref, other_ref)):
                x = ref[pos, :rows, :]
                place = (pl.ds(arc * rows, rows), pl.ds(c * t, t))
                flat_ref[place] = x
                weighted_ref[place] = (x.astype(F32) * w_ref[pl.ds(arc * rows, rows), :]).astype(BF16)

    def columns(entry):
        return pl.ds(pl.multiple_of(pairs_ref[2 * pl.program_id(0) + entry] * WIDE, WIDE), WIDE)

    def product(x, y):
        return lax.dot_general(x, y, (((0,), (0,)), ((), ())), preferred_element_type=F32)

    i, j = columns(0), columns(1)
    s_ref[0] = 0.5 * (
        product(flat_ref[:, i], weighted_ref[:, j]) + product(weighted_ref[:, i], flat_ref[:, j])
    )


def lead_blocks(own, other, weight_columns, order, rows):
    n, padded, t = own.shape
    width = n * t
    count = len(PAIRS[0])
    pairs = jnp.array(PAIRS, jnp.int32).reshape(2, 2 * count)[lax.axis_index("arc")]
    whole = pl.BlockSpec((n, padded, t), lambda s, p: (0, 0, 0))
    return pl.pallas_call(
        functools.partial(lead_kernel, order, rows),
        grid_spec=pltpu.PrefetchScalarGridSpec(
            num_scalar_prefetch=1,
            grid=(count,),
            in_specs=[whole, whole, pl.BlockSpec((2 * rows, t), lambda s, p: (0, 0))],
            out_specs=(
                pl.BlockSpec((2 * rows, width), lambda s, p: (0, 0)),
                pl.BlockSpec((1, WIDE, WIDE), lambda s, p: (s, 0, 0)),
            ),
            scratch_shapes=[pltpu.VMEM((2 * rows, width), BF16)],
        ),
        out_shape=(
            jax.ShapeDtypeStruct((2 * rows, width), BF16),
            jax.ShapeDtypeStruct((count, WIDE, WIDE), F32),
        ),
        compiler_params=pltpu.CompilerParams(vmem_limit_bytes=52 * 1024 * 1024),
        cost_estimate=SHORT,
        name="lead_blocks",
    )(pairs, own, other, weight_columns)


def assemble_kernel(table_ref, mine_ref, theirs_ref, late_ref, late_other_ref, prior_ref, out_ref):
    i, j = pl.program_id(0), pl.program_id(1)
    entry = table_ref[4 * i + j]
    at = entry % 8
    block = jnp.where(entry < 8, mine_ref[at] + late_ref[at], theirs_ref[at] + late_other_ref[at])

    @pl.when(i < j)
    def _():
        out_ref[...] = block

    @pl.when(i > j)
    def _():
        out_ref[...] = block.T

    @pl.when(i == j)
    def _():
        x = lax.broadcasted_iota(jnp.int32, block.shape, 0)
        y = lax.broadcasted_iota(jnp.int32, block.shape, 1)
        out_ref[...] = block + jnp.where(x == y, prior_ref[...], 0.0)


def assemble(mine, theirs, late, late_other, priors, *wait):
    width = priors.shape[0]
    tables = [[0] * 16, [0] * 16]
    for core in range(2):
        for slot, (i, j) in enumerate(PAIRS[core]):
            for a in range(2):
                tables[a][4 * i + j] = tables[a][4 * j + i] = slot + (0 if a == core else 8)
    table = after(jnp.array(tables, jnp.int32)[lax.axis_index("arc")], *wait)
    blocks = pl.BlockSpec(mine.shape, lambda i, j, p: (0, 0, 0))
    return pl.pallas_call(
        assemble_kernel,
        grid_spec=pltpu.PrefetchScalarGridSpec(
            num_scalar_prefetch=1,
            grid=(4, 4),
            in_specs=[blocks] * 4 + [pl.BlockSpec((1, WIDE), lambda i, j, p: (0, j))],
            out_specs=pl.BlockSpec((WIDE, WIDE), lambda i, j, p: (i, j)),
        ),
        out_shape=jax.ShapeDtypeStruct((width, width), F32),
        compiler_params=pltpu.CompilerParams(vmem_limit_bytes=24 * 1024 * 1024),
        cost_estimate=SHORT,
        name="assemble",
    )(table, mine, theirs, late, late_other, priors[None])


def finish_kernel(top, halved, kc, q, n_row, base, step, here_ref, *refs):
    sums, refs = refs[:4], refs[4:]
    if top:
        square_ref, refs = refs[0], refs[1:]
    hi_ref, lo_ref, prior_ref = refs[:3]
    normal_ref, panel_ref, parts = refs[-3:]
    a, r, c = here_ref[0], here_ref[1], here_ref[2]
    g = pl.program_id(0)
    t = prior_ref.shape[1]
    k = base + step * g
    odd = r % 2
    size = q * t
    x = lax.broadcasted_iota(jnp.int32, (t, t), 0)
    y = lax.broadcasted_iota(jnp.int32, (t, t), 1)

    for z in range(q):
        at = jnp.where(odd == 1, q - 1 - z, z)
        core, index = (at // (q // 2), at % (q // 2)) if halved else (g, at)
        use = core == a

        def total(columns):
            keep, keep_other, late, late_other = [ref[index, :, columns] for ref in sums]
            return jnp.where(use, keep, keep_other) + jnp.where(use, late, late_other).astype(F32)

        rows = total(slice(0, kc * t))
        for k2 in range(kc):
            tile = rows[:, k2 * t : (k2 + 1) * t]
            same = jnp.logical_and(k == k2, c == z * n_row + r)
            tile = tile + jnp.where(jnp.logical_and(same, x == y), prior_ref[k2 : k2 + 1, :], 0.0)
            normal_ref[pl.ds(z * t * kc + k2, t, stride=kc), :] = tile
        if top:
            first = pl.multiple_of((z * n_row + r) * t, t)
            rows = square_ref[pl.ds(first, t), :]
        else:
            rows = total(slice(kc * t, None))
        high = rows.astype(BF16)
        parts[z * t : (z + 1) * t, :] = high
        parts[size + z * t : size + (z + 1) * t, :] = (rows - high.astype(F32)).astype(BF16)

    def product(u, v):
        return lax.dot_general(u, v, (((1,), (1,)), ((), ())), preferred_element_type=F32)

    width = panel_ref.shape[1]
    for lo in range(0, width, WIDE):
        hi = lo + WIDE
        both = product(parts[:, :hi], hi_ref[lo:hi, :hi])
        panel_ref[:, lo:hi] = (
            both[:size] + both[size:] + product(parts[:size, :hi], lo_ref[lo:hi, :hi])
        )


def finish(outputs, here, sums, square, inverse, prior, halved, base, step, count, kc, q, n_row):
    t = prior.shape[1]
    width = inverse[0].shape[0]
    top = len(square) == 1
    arrays = [*sums, *square, *inverse, prior]

    def spec(x):
        if x.ndim == 3:
            return pl.BlockSpec(x.shape, lambda g, p: (0, 0, 0), pipeline_mode=pl.Buffered(1))
        return pl.BlockSpec(x.shape, lambda g, p: (0, 0), pipeline_mode=pl.Buffered(1))

    shapes = (
        jax.ShapeDtypeStruct((kc * q * t * kc, t), F32),
        jax.ShapeDtypeStruct((kc * q * t, width), F32),
    )
    n_in = 1 + len(arrays)

    def place(g, p):
        return (base + step * g, 0)

    return pl.pallas_call(
        functools.partial(finish_kernel, top, halved, kc, q, n_row, base, step),
        grid_spec=pltpu.PrefetchScalarGridSpec(
            num_scalar_prefetch=1,
            grid=(count,),
            in_specs=[spec(x) for x in arrays] + [pl.BlockSpec(memory_space=pl.ANY)] * len(outputs),
            out_specs=(pl.BlockSpec((q * t * kc, t), place), pl.BlockSpec((q * t, width), place)),
            scratch_shapes=[pltpu.VMEM((2 * q * t, width), BF16)],
        ),
        out_shape=shapes,
        input_output_aliases={n_in: 0, n_in + 1: 1} if outputs else {},
        compiler_params=pltpu.CompilerParams(vmem_limit_bytes=32 * 1024 * 1024),
        cost_estimate=pl.CostEstimate(
            flops=count * 6 * 10**9, bytes_accessed=count * 8 * 10**6, transcendentals=0
        ),
        name=f"finish_{base}",
    )(here, *arrays, *outputs)


def finish_fast(prior, leading, gathered, weights):
    packed, arrived, priors = leading
    lead_own, lead_other, main, rest = gathered
    kc, t = prior.shape
    n_row = lax.axis_size("row")
    q = lax.axis_size("col") // n_row
    m = len(main)
    a, r, c = [lax.axis_index(x) for x in ("arc", "row", "col")]
    here = jnp.stack([a, r, c]).astype(jnp.int32)
    half = q // 2

    def pair(x):
        return [x, swap(x, "arc")]

    def rows_of(keep, late):
        return pair(keep) + pair(late)

    wide = lax.optimization_barrier(jnp.concatenate(weights, axis=1))
    rows = wide.shape[0] // 2
    other_owner = (r + 1) % n_row

    def product(blocks, place, w, dtype, *wait):
        x = lax.dynamic_index_in_dim(blocks, after(place, *wait), 0, keepdims=False)
        total = jnp.einsum("qrt,ru->qtu", x, w, preferred_element_type=F32)
        return lax.optimization_barrier(total.astype(dtype))

    def half_products(own, other, w, *wait):
        mine = core_half(by_owner(own), after(a, *wait))
        x = jnp.concatenate([mine[:, :, :rows], other[:, :, :rows]], axis=2)
        total = jnp.einsum("oqrt,ru->oqtu", x, w, preferred_element_type=F32)
        total = lax.optimization_barrier(total)
        send = lax.dynamic_index_in_dim(total, other_owner, 0, keepdims=False).astype(BF16)
        return send, lax.dynamic_index_in_dim(total, r, 0, keepdims=False)

    x = core_half(by_owner(lead_other), a)
    lead_sent, lead_keep = half_products(lead_own, x, wide[:, : kc * t], packed)
    lead_late = swap(lead_sent, "row")
    main = [by_owner(x) for x in main]
    blocks = pair(packed) + pair(arrived)
    sent = product(main[0], other_owner, wide, BF16, lead_keep, blocks[3])
    late = [swap(sent, "row")]
    symmetric = assemble(*blocks, priors, sent, lead_late)

    ahead = {7: late}
    for state in inverse_cholesky_steps(symmetric, ahead):
        pass
    high = lax.reduce_precision(state[1], 8, 7)
    inverse = (high.astype(BF16), (state[1] - high).astype(BF16))
    inverse = lax.optimization_barrier(inverse)

    wait = inverse[1]
    begun = []
    for i in range(1, m):
        wait = product(main[i], other_owner, wide, BF16, wait)
        pieces = [swap(wait[:half], "row"), swap(wait[half:], "row")]
        begun.append(pieces)
        late.append(jnp.concatenate(pieces))
    kept = [product(main[0], r, wide, F32, wait)]
    args = (inverse, prior)
    shape = (kc, q, n_row)
    gate = after(here, kept[0])
    out = finish([], gate, rows_of(lead_keep, lead_late), [symmetric], *args, True, 0, 1, 1, *shape)
    wait = out[1]
    for i in range(1, m):
        wait = product(main[i], r, wide, F32, wait)
        kept.append(wait)
    rest_kept = []
    for x in rest:
        received = swap(core_half(by_owner(x), after(1 - a, wait, *[x[0] for x in begun])), "arc")
        sent, keep = half_products(x, received, wide, wait)
        late.append(swap(sent, "row"))
        rest_kept.append(keep)
        wait = sent
    zero = after(jnp.int32(0), wait)
    gate = after(here, wait, *[lax.dynamic_slice(x[1], (zero, 0, 0), (1, 1, 1)) for x in begun])
    out = finish(out, gate, rows_of(kept[0], late[0]), [], *args, False, 1, m, 2, *shape)
    zero = after(jnp.int32(0), out[1])
    late[m:] = [lax.dynamic_slice(x, (zero, 0, 0), x.shape) for x in late[m:]]
    kept += rest_kept
    chunks = [(1 + i, m, 2, False) for i in range(m)]
    chunks += [(1 + 2 * m + i, 1, 1, True) for i in range(len(rest))]
    for (base, step, count, halved), keep, x in list(zip(chunks, kept, late))[1:]:
        out = finish(out, gate, rows_of(keep, x), [], *args, halved, base, step, count, *shape)
    normal, panel = out
    return (normal.reshape(kc * q, 1, t, kc, 1, t), panel.reshape(kc * q, 1, t, -1))


def body(design, obs_weight, prior):
    n_row = lax.axis_size("row")
    n_col = lax.axis_size("col")
    a = lax.axis_index("arc")
    r = lax.axis_index("row")
    c = lax.axis_index("col")
    rows, kc, _, t = design.shape
    q = n_col // n_row
    m = (kc - 1) // 2
    width = n_col * t
    first = a == 0
    fast = t == 128 and width == 4 * WIDE and n_row == 2
    order = ring_order(n_col, n_row)
    own = lax.optimization_barrier(jnp.transpose(design[:, :, 0, :], (1, 0, 2)))

    extra = jnp.concatenate([p[None] for p in split3(prior[0, 0])] + [jnp.zeros((13, t), BF16)])
    lead_in = lax.pad(design[:, 0, 0, :], BF16(0), ((0, 16, 0), (0, 0, 0)))
    lead_in = lead_in + lax.pad(extra, BF16(0), ((rows, 0, 0), (0, 0, 0)))
    lead_all = gather_cols(lead_in, order)
    other = swap(own, "arc")
    weight_other = swap(obs_weight, "arc")
    both = jnp.concatenate([own, other], axis=1)
    w2 = jnp.concatenate([obs_weight, weight_other])
    weighted = jnp.transpose(weigh(both, w2), (1, 0, 2)).reshape(2 * rows, kc * t)
    weighted = lax.optimization_barrier(weighted)

    def hold(x, *others):
        return lax.optimization_barrier((x, others))[0]

    shares = [lax.dynamic_index_in_dim(both, 1 + m * a + i, 0, keepdims=False) for i in range(m)]
    shares = list(lax.optimization_barrier(tuple(shares)))
    weight_columns = jnp.broadcast_to(w2[:, None], (2 * rows, t))
    main = [gather_cols(shares[0], order)]
    lead_own = hold(lead_all, shares, weighted, weight_columns)
    shares = [hold(x, lead_own) for x in shares[1:]]
    main += [gather_cols(x, order) for x in shares]
    lead_other = swap(lead_own, "arc")
    priors = jnp.sum(lead_own[:, rows : rows + 3].astype(F32), axis=1)
    priors = jnp.concatenate([priors[order.index(x)] for x in range(n_col)])

    if fast:
        lead_weighted, packed = lead_blocks(
            lead_own, lead_other, weight_columns, order, rows
        )
        arrived = swap(packed, "row")
        first_use = packed
    else:
        flat = jnp.concatenate([lead_own[:, :rows], lead_other[:, :rows]], axis=1)
        flat = jnp.stack([flat[order.index(x)] for x in range(n_col)])
        lead_weighted = jnp.transpose(weigh(flat, w2), (1, 0, 2)).reshape(2 * rows, width)
        first_use = lead_weighted
        half = n_col // 2
        square = jnp.einsum(
            "crt,ru->ctu",
            lax.dynamic_slice_in_dim(flat, half * a, half, 0),
            lead_weighted,
            preferred_element_type=F32,
        )
        square = lax.psum(square, "row")
        square_other = swap(square, "arc")
        square = jnp.concatenate(
            [jnp.where(first, square, square_other), jnp.where(first, square_other, square)]
        ).reshape(width, width)
        symmetric = 0.5 * (square + square.T) + jnp.diag(priors)
    rest = [gather_cols(hold(x, first_use, shares), order) for x in own[1 + 2 * m :]]

    if fast:
        return finish_fast(
            prior.reshape(kc, t),
            (packed, arrived, priors),
            (lead_own, lead_other, main, rest),
            (weighted, lead_weighted),
        )

    halves = [core_half(by_owner(x[:, :rows]), a) for x in (lead_own, lead_other)]
    split = (weighted[:rows], weighted[rows:])
    lead_split = (lead_weighted[:rows], lead_weighted[rows:])
    n_lead = partial_sums(halves, split)
    main_sums = [partial_sums([by_owner(x)], [weighted], [lead_weighted]) for x in main]
    rest_sums = [partial_sums(core_halves(by_owner(x)), split, lead_split) for x in rest]
    *_, (_, inverse) = inverse_cholesky_steps(symmetric, {})

    def sides(x):
        y = swap(x, "arc")
        return jnp.where(first, x, y), jnp.where(first, y, x)

    n_rows, p_rows = [None] * kc, [None] * kc
    n_rows[0] = jnp.concatenate(sides(n_lead[0]))
    for i, (n, p) in enumerate(main_sums):
        n_rows[1 + i], n_rows[1 + m + i] = sides(n)
        p_rows[1 + i], p_rows[1 + m + i] = sides(p)
    for i, (n, p) in enumerate(rest_sums):
        n_rows[1 + 2 * m + i] = jnp.concatenate(sides(n))
        p_rows[1 + 2 * m + i] = jnp.concatenate(sides(p))

    def in_order(x):
        x = jnp.stack(x)
        return jnp.where(r % 2 == 1, x[:, ::-1], x)

    tiles = in_order(n_rows).reshape(kc * q, t, kc, t)
    tile_rows = jnp.arange(kc * q, dtype=jnp.int32) * n_row + r
    tile_cols = jnp.arange(kc, dtype=jnp.int32) * n_col + c
    same = (tile_rows[:, None] == tile_cols[None, :]).astype(F32)
    identity = jnp.eye(t, dtype=F32)
    added = same[:, None, :, None] * identity[None, :, None, :] * prior.reshape(kc, t)[None, None]
    normal = (tiles + added).reshape(kc * q, 1, t, kc, 1, t)
    top = lax.dynamic_index_in_dim(symmetric.reshape(q, n_row, t, width), r, 1, keepdims=False)
    panel_rows = jnp.concatenate([top[None], in_order(p_rows[1:])])
    result = jnp.einsum(
        "rk,jk->rj",
        panel_rows.reshape(kc * q * t, width),
        inverse,
        precision=lax.Precision.HIGH,
        preferred_element_type=F32,
    )
    return (normal, result.reshape(kc * q, 1, t, width))


def solution(mesh):
    placed = (P(("arc", "row"), None, "col", None), P(("arc", "row")), P(None, "col", None))
    return jax.shard_map(
        body,
        mesh=mesh,
        in_specs=placed,
        out_specs=(P(None, "row", None, None, "col", None), P(None, "row", None, None)),
        check_vma=False,
    )
```

```python
import functools

import jax
import jax.numpy as jnp
from jax import lax
from jax.experimental import pallas as pl
from jax.experimental.pallas import tpu as pltpu
from jax.sharding import PartitionSpec as P

F32 = jnp.float32
BF16 = jnp.bfloat16

SHORT = pl.CostEstimate(flops=10**6, bytes_accessed=10**5, transcendentals=0)
BLOCK = 128
STRIP = 16


def dot_tn(x, y):
    return lax.dot_general(
        x, y, (((0,), (0,)), ((), ())), precision=lax.Precision.HIGHEST, preferred_element_type=F32
    )


def dot_nn(x, y):
    return jnp.dot(x, y, precision=lax.Precision.HIGHEST, preferred_element_type=F32)


def inverse_factor(square):
    n = square.shape[0]
    count = n // STRIP
    row_id = lax.broadcasted_iota(jnp.int32, (STRIP, n), 0)
    left = [square[i * STRIP : (i + 1) * STRIP, :] for i in range(count)]
    lane = lax.broadcasted_iota(jnp.int32, (STRIP, n), 1)
    right = [(lane == row_id + i * STRIP).astype(F32) for i in range(count)]
    done = []
    for b in range(count):
        ps, pe = left[b], right[b]
        columns = [
            jnp.broadcast_to(ps[:, b * STRIP + l : b * STRIP + l + 1], (STRIP, n))
            for l in range(STRIP)
        ]
        scale = jnp.zeros((STRIP, n), F32)
        for j in range(STRIP):
            rs = lax.rsqrt(columns[j][j : j + 1, :])
            col = columns[j] * rs
            below = jnp.where(row_id > j, col, 0.0)
            ps = ps - below * (ps[j : j + 1, :] * rs)
            pe = pe - below * (pe[j : j + 1, :] * rs)
            for l in range(j + 1, STRIP):
                columns[l] = columns[l] - col * (columns[l][j : j + 1, :] * rs)
            scale = jnp.where(row_id == j, rs, scale)
        ps = ps * scale
        pe = pe * scale
        done.append(pe)
        if b + 1 < count:
            update = dot_tn(ps, jnp.concatenate([ps, pe], axis=1))
            for i in range(b + 1, count):
                left[i] = left[i] - update[i * STRIP : (i + 1) * STRIP, :n]
                right[i] = right[i] - update[i * STRIP : (i + 1) * STRIP, n:]
    return jnp.concatenate(done, axis=0)


def factor_step(k, blocks, s_ref, *refs):
    lo, hi = k * BLOCK, (k + 1) * BLOCK
    u_out, e_out = refs[-2:]
    if k:
        u_ref, e_ref = refs[:2]
        above = u_ref[:, lo:hi]
        diag = s_ref[:, lo:hi] - dot_tn(above, above)
    else:
        diag = s_ref[:, lo:hi]
    inverse = inverse_factor(diag)
    width = blocks * BLOCK
    u_out[:, :hi] = jnp.zeros((BLOCK, hi), F32)
    if k + 1 < blocks:
        rest = s_ref[:, hi:]
        if k:
            rest = rest - dot_tn(above, u_ref[:, hi:])
        u_out[:, hi:] = dot_nn(inverse, rest)
        e_out[:, hi:] = jnp.zeros((BLOCK, width - hi), F32)
    if k:
        e_out[:, :lo] = -dot_nn(inverse, dot_tn(above, e_ref[:, :lo]))
    e_out[:, lo:hi] = inverse


def inverse_cholesky_steps(square, ahead):
    width = square.shape[0]
    blocks = width // BLOCK
    shape = jax.ShapeDtypeStruct((width, width), F32)
    state = None
    for k in range(blocks):
        gates = []
        if k in ahead:
            gate = after(jnp.zeros((1,), jnp.int32), *ahead[k])
            gates = [gate]
        row = pl.BlockSpec((BLOCK, width), lambda i, k=k: (k, 0))
        seen = pl.BlockSpec((k * BLOCK, width), lambda i: (0, 0))
        state = pl.pallas_call(
            functools.partial(factor_step, k, blocks),
            grid=(1,),
            out_shape=(shape, shape),
            in_specs=[row]
            + ([seen, seen] if k else [])
            + [pl.BlockSpec(memory_space=pltpu.SMEM)] * len(gates),
            out_specs=(row, row),
            input_output_aliases={1: 0, 2: 1} if k else {},
            compiler_params=pltpu.CompilerParams(vmem_limit_bytes=24 * 1024 * 1024),
            cost_estimate=SHORT,
            name=f"factor_{k}",
        )(square, *(state or ()), *gates)
        yield state


def ring_order(n, owners):
    order = []
    for owner in range(owners):
        order += list(range(owner, n, owners))[:: -1 if owner % 2 else 1]
    return order


def swap(x, axis, shift=1):
    n = lax.axis_size(axis)
    return lax.ppermute(x, axis, [(i, (i + shift) % n) for i in range(n)])


def after(index, *others):
    for x in others:
        one = lax.slice(x, (0,) * x.ndim, (1,) * x.ndim).reshape(()).astype(F32)
        index = index + jnp.minimum(jnp.abs(one), 0.0).astype(jnp.int32)
    return index


def gather_cols(x, order):
    return lax.all_gather(x, "col", axis=0, tiled=False, axis_index_groups=[order])


def weigh(x, w):
    return (x.astype(F32) * w[:, None]).astype(BF16)


def split3(x):
    hi = lax.reduce_precision(x, 8, 7)
    mid = lax.reduce_precision(x - hi, 8, 7)
    return [y.astype(BF16) for y in (hi, mid, x - hi - mid)]


def by_owner(x):
    n_row = lax.axis_size("row")
    return x.reshape((n_row, x.shape[0] // n_row) + x.shape[1:])


def product_of(blocks, owner, group):
    total = 0.0
    for x, w in zip(blocks, group):
        mine = lax.dynamic_index_in_dim(x, owner, 0, keepdims=False)
        total += jnp.einsum("qrt,ru->qtu", mine, w, preferred_element_type=F32)
    return total


def sends(blocks, groups, *wait):
    n_row = lax.axis_size("row")
    r = after(lax.axis_index("row"), *wait)
    parts = [
        [product_of(blocks, (r + d) % n_row, w).astype(BF16) for d in range(1, n_row)]
        for w in groups
    ]
    return lax.optimization_barrier(parts)


def keeps(blocks, groups, *wait):
    r = after(lax.axis_index("row"), *wait)
    return lax.optimization_barrier([product_of(blocks, r, w) for w in groups])


def receive(sent):
    return [[swap(x, "row", 1 + i) for i, x in enumerate(parts)] for parts in sent]


def partial_sums(blocks, *groups):
    totals = []
    for total, parts in zip(keeps(blocks, groups), receive(sends(blocks, groups))):
        for x in parts:
            total = total + x.astype(F32)
        totals.append(total)
    return totals


def core_half(x, core):
    half = x.shape[1] // 2
    return lax.dynamic_slice_in_dim(x, half * core, half, 1)


def core_halves(x):
    a = lax.axis_index("arc")
    return [core_half(x, a), swap(core_half(x, 1 - a), "arc")]


PAIRS = (((0, 0), (0, 1), (0, 2), (0, 3), (3, 3)), ((1, 1), (1, 2), (1, 3), (2, 2), (2, 3)))
WIDE = 256


def lead_kernel(order, rows, pairs_ref, own_ref, other_ref, w_ref, weighted_ref, s_ref, flat_ref):
    @pl.when(pl.program_id(0) == 0)
    def _():
        t = own_ref.shape[2]
        for pos, c in enumerate(order):
            for arc, ref in enumerate((own_ref, other_ref)):
                x = ref[pos, :rows, :]
                place = (pl.ds(arc * rows, rows), pl.ds(c * t, t))
                flat_ref[place] = x
                weighted_ref[place] = (x.astype(F32) * w_ref[pl.ds(arc * rows, rows), :]).astype(BF16)

    def columns(entry):
        return pl.ds(pl.multiple_of(pairs_ref[2 * pl.program_id(0) + entry] * WIDE, WIDE), WIDE)

    def product(x, y):
        return lax.dot_general(x, y, (((0,), (0,)), ((), ())), preferred_element_type=F32)

    i, j = columns(0), columns(1)
    s_ref[0] = 0.5 * (
        product(flat_ref[:, i], weighted_ref[:, j]) + product(weighted_ref[:, i], flat_ref[:, j])
    )


def lead_blocks(own, other, weight_columns, order, rows):
    n, padded, t = own.shape
    width = n * t
    count = len(PAIRS[0])
    pairs = jnp.array(PAIRS, jnp.int32).reshape(2, 2 * count)[lax.axis_index("arc")]
    whole = pl.BlockSpec((n, padded, t), lambda s, p: (0, 0, 0))
    return pl.pallas_call(
        functools.partial(lead_kernel, order, rows),
        grid_spec=pltpu.PrefetchScalarGridSpec(
            num_scalar_prefetch=1,
            grid=(count,),
            in_specs=[whole, whole, pl.BlockSpec((2 * rows, t), lambda s, p: (0, 0))],
            out_specs=(
                pl.BlockSpec((2 * rows, width), lambda s, p: (0, 0)),
                pl.BlockSpec((1, WIDE, WIDE), lambda s, p: (s, 0, 0)),
            ),
            scratch_shapes=[pltpu.VMEM((2 * rows, width), BF16)],
        ),
        out_shape=(
            jax.ShapeDtypeStruct((2 * rows, width), BF16),
            jax.ShapeDtypeStruct((count, WIDE, WIDE), F32),
        ),
        compiler_params=pltpu.CompilerParams(vmem_limit_bytes=52 * 1024 * 1024),
        cost_estimate=SHORT,
        name="lead_blocks",
    )(pairs, own, other, weight_columns)


def assemble_kernel(table_ref, mine_ref, theirs_ref, late_ref, late_other_ref, prior_ref, out_ref):
    i, j = pl.program_id(0), pl.program_id(1)
    entry = table_ref[4 * i + j]
    at = entry % 8
    block = jnp.where(entry < 8, mine_ref[at] + late_ref[at], theirs_ref[at] + late_other_ref[at])

    @pl.when(i < j)
    def _():
        out_ref[...] = block

    @pl.when(i > j)
    def _():
        out_ref[...] = block.T

    @pl.when(i == j)
    def _():
        x = lax.broadcasted_iota(jnp.int32, block.shape, 0)
        y = lax.broadcasted_iota(jnp.int32, block.shape, 1)
        out_ref[...] = block + jnp.where(x == y, prior_ref[...], 0.0)


def assemble(mine, theirs, late, late_other, priors, *wait):
    width = priors.shape[0]
    tables = [[0] * 16, [0] * 16]
    for core in range(2):
        for slot, (i, j) in enumerate(PAIRS[core]):
            for a in range(2):
                tables[a][4 * i + j] = tables[a][4 * j + i] = slot + (0 if a == core else 8)
    table = after(jnp.array(tables, jnp.int32)[lax.axis_index("arc")], *wait)
    blocks = pl.BlockSpec(mine.shape, lambda i, j, p: (0, 0, 0))
    return pl.pallas_call(
        assemble_kernel,
        grid_spec=pltpu.PrefetchScalarGridSpec(
            num_scalar_prefetch=1,
            grid=(4, 4),
            in_specs=[blocks] * 4 + [pl.BlockSpec((1, WIDE), lambda i, j, p: (0, j))],
            out_specs=pl.BlockSpec((WIDE, WIDE), lambda i, j, p: (i, j)),
        ),
        out_shape=jax.ShapeDtypeStruct((width, width), F32),
        compiler_params=pltpu.CompilerParams(vmem_limit_bytes=24 * 1024 * 1024),
        cost_estimate=SHORT,
        name="assemble",
    )(table, mine, theirs, late, late_other, priors[None])


def finish_kernel(top, halved, kc, q, n_row, base, step, here_ref, *refs):
    sums, refs = refs[:4], refs[4:]
    if top:
        square_ref, refs = refs[0], refs[1:]
    hi_ref, lo_ref, prior_ref = refs[:3]
    normal_ref, panel_ref, parts = refs[-3:]
    a, r, c = here_ref[0], here_ref[1], here_ref[2]
    g = pl.program_id(0)
    t = prior_ref.shape[1]
    k = base + step * g
    odd = r % 2
    size = q * t
    x = lax.broadcasted_iota(jnp.int32, (t, t), 0)
    y = lax.broadcasted_iota(jnp.int32, (t, t), 1)

    for z in range(q):
        at = jnp.where(odd == 1, q - 1 - z, z)
        core, index = (at // (q // 2), at % (q // 2)) if halved else (g, at)
        use = core == a

        def total(columns):
            keep, keep_other, late, late_other = [ref[index, :, columns] for ref in sums]
            return jnp.where(use, keep, keep_other) + jnp.where(use, late, late_other).astype(F32)

        rows = total(slice(0, kc * t))
        for k2 in range(kc):
            tile = rows[:, k2 * t : (k2 + 1) * t]
            same = jnp.logical_and(k == k2, c == z * n_row + r)
            tile = tile + jnp.where(jnp.logical_and(same, x == y), prior_ref[k2 : k2 + 1, :], 0.0)
            normal_ref[pl.ds(z * t * kc + k2, t, stride=kc), :] = tile
        if top:
            first = pl.multiple_of((z * n_row + r) * t, t)
            rows = square_ref[pl.ds(first, t), :]
        else:
            rows = total(slice(kc * t, None))
        high = rows.astype(BF16)
        parts[z * t : (z + 1) * t, :] = high
        parts[size + z * t : size + (z + 1) * t, :] = (rows - high.astype(F32)).astype(BF16)

    def product(u, v):
        return lax.dot_general(u, v, (((1,), (1,)), ((), ())), preferred_element_type=F32)

    width = panel_ref.shape[1]
    for lo in range(0, width, WIDE):
        hi = lo + WIDE
        both = product(parts[:, :hi], hi_ref[lo:hi, :hi])
        panel_ref[:, lo:hi] = (
            both[:size] + both[size:] + product(parts[:size, :hi], lo_ref[lo:hi, :hi])
        )


def finish(outputs, here, sums, square, inverse, prior, halved, base, step, count, kc, q, n_row):
    t = prior.shape[1]
    width = inverse[0].shape[0]
    top = len(square) == 1
    arrays = [*sums, *square, *inverse, prior]

    def spec(x):
        if x.ndim == 3:
            return pl.BlockSpec(x.shape, lambda g, p: (0, 0, 0), pipeline_mode=pl.Buffered(1))
        return pl.BlockSpec(x.shape, lambda g, p: (0, 0), pipeline_mode=pl.Buffered(1))

    shapes = (
        jax.ShapeDtypeStruct((kc * q * t * kc, t), F32),
        jax.ShapeDtypeStruct((kc * q * t, width), F32),
    )
    n_in = 1 + len(arrays)

    def place(g, p):
        return (base + step * g, 0)

    return pl.pallas_call(
        functools.partial(finish_kernel, top, halved, kc, q, n_row, base, step),
        grid_spec=pltpu.PrefetchScalarGridSpec(
            num_scalar_prefetch=1,
            grid=(count,),
            in_specs=[spec(x) for x in arrays] + [pl.BlockSpec(memory_space=pl.ANY)] * len(outputs),
            out_specs=(pl.BlockSpec((q * t * kc, t), place), pl.BlockSpec((q * t, width), place)),
            scratch_shapes=[pltpu.VMEM((2 * q * t, width), BF16)],
        ),
        out_shape=shapes,
        input_output_aliases={n_in: 0, n_in + 1: 1} if outputs else {},
        compiler_params=pltpu.CompilerParams(vmem_limit_bytes=32 * 1024 * 1024),
        cost_estimate=pl.CostEstimate(
            flops=count * 6 * 10**9, bytes_accessed=count * 8 * 10**6, transcendentals=0
        ),
        name=f"finish_{base}",
    )(here, *arrays, *outputs)


def finish_fast(prior, leading, gathered, weights):
    packed, arrived, priors = leading
    lead_own, lead_other, main, rest = gathered
    kc, t = prior.shape
    n_row = lax.axis_size("row")
    q = lax.axis_size("col") // n_row
    m = len(main)
    a, r, c = [lax.axis_index(x) for x in ("arc", "row", "col")]
    here = jnp.stack([a, r, c]).astype(jnp.int32)
    half = q // 2

    def pair(x):
        return [x, swap(x, "arc")]

    def rows_of(keep, late):
        return pair(keep) + pair(late)

    wide = lax.optimization_barrier(jnp.concatenate(weights, axis=1))
    rows = wide.shape[0] // 2
    other_owner = (r + 1) % n_row

    def product(blocks, place, w, dtype, *wait):
        x = lax.dynamic_index_in_dim(blocks, after(place, *wait), 0, keepdims=False)
        total = jnp.einsum("qrt,ru->qtu", x, w, preferred_element_type=F32)
        return lax.optimization_barrier(total.astype(dtype))

    def half_products(own, other, w, *wait):
        mine = core_half(by_owner(own), after(a, *wait))
        x = jnp.concatenate([mine[:, :, :rows], other[:, :, :rows]], axis=2)
        total = jnp.einsum("oqrt,ru->oqtu", x, w, preferred_element_type=F32)
        total = lax.optimization_barrier(total)
        send = lax.dynamic_index_in_dim(total, other_owner, 0, keepdims=False).astype(BF16)
        return send, lax.dynamic_index_in_dim(total, r, 0, keepdims=False)

    x = core_half(by_owner(lead_other), a)
    lead_sent, lead_keep = half_products(lead_own, x, wide[:, : kc * t], packed)
    lead_late = swap(lead_sent, "row")
    main = [by_owner(x) for x in main]
    blocks = pair(packed) + pair(arrived)
    sent = product(main[0], other_owner, wide, BF16, lead_keep, lead_late, blocks[3])
    late = [swap(sent, "row")]
    symmetric = assemble(*blocks, priors, sent)

    ahead = {7: late}
    for state in inverse_cholesky_steps(symmetric, ahead):
        pass
    high = lax.reduce_precision(state[1], 8, 7)
    inverse = (high.astype(BF16), (state[1] - high).astype(BF16))
    inverse = lax.optimization_barrier(inverse)

    wait = inverse[1]
    for i in range(1, m):
        wait = product(main[i], other_owner, wide, BF16, wait)
        late.append(swap(wait, "row"))
    kept = [product(main[0], r, wide, F32, wait)]
    args = (inverse, prior)
    shape = (kc, q, n_row)
    gate = after(here, kept[0])
    out = finish([], gate, rows_of(lead_keep, lead_late), [symmetric], *args, True, 0, 1, 1, *shape)
    wait = out[1]
    for i in range(1, m):
        wait = product(main[i], r, wide, F32, wait)
        kept.append(wait)
    rest_kept = []
    for x in rest:
        received = swap(core_half(by_owner(x), after(1 - a, wait, *late[1:m])), "arc")
        sent, keep = half_products(x, received, wide, wait)
        late.append(swap(sent, "row"))
        rest_kept.append(keep)
        wait = sent
    gate = after(here, wait)
    out = finish(out, gate, rows_of(kept[0], late[0]), [], *args, False, 1, m, 2, *shape)
    for i in range(1, m):
        out = finish(out, gate, rows_of(kept[i], late[i]), [], *args, False, 1 + i, m, 2, *shape)
    zero = after(jnp.int32(0), out[1]).astype(BF16)
    for i, (keep, x) in enumerate(zip(rest_kept, late[m:])):
        sums = rows_of(keep, x + zero)
        out = finish(out, gate, sums, [], *args, True, 1 + 2 * m + i, 1, 1, *shape)
    normal, panel = out
    return (normal.reshape(kc * q, 1, t, kc, 1, t), panel.reshape(kc * q, 1, t, -1))


def body(design, obs_weight, prior):
    n_row = lax.axis_size("row")
    n_col = lax.axis_size("col")
    a = lax.axis_index("arc")
    r = lax.axis_index("row")
    c = lax.axis_index("col")
    rows, kc, _, t = design.shape
    q = n_col // n_row
    m = (kc - 1) // 2
    width = n_col * t
    first = a == 0
    fast = t == 128 and width == 4 * WIDE and n_row == 2
    order = ring_order(n_col, n_row)
    own = lax.optimization_barrier(jnp.transpose(design[:, :, 0, :], (1, 0, 2)))

    extra = jnp.concatenate([p[None] for p in split3(prior[0, 0])] + [jnp.zeros((13, t), BF16)])
    lead_in = lax.pad(design[:, 0, 0, :], BF16(0), ((0, 16, 0), (0, 0, 0)))
    lead_in = lead_in + lax.pad(extra, BF16(0), ((rows, 0, 0), (0, 0, 0)))
    lead_all = gather_cols(lead_in, order)
    other = swap(own, "arc")
    weight_other = swap(obs_weight, "arc")
    both = jnp.concatenate([own, other], axis=1)
    w2 = jnp.concatenate([obs_weight, weight_other])
    weighted = jnp.transpose(weigh(both, w2), (1, 0, 2)).reshape(2 * rows, kc * t)
    weighted = lax.optimization_barrier(weighted)

    def hold(x, *others):
        return lax.optimization_barrier((x, others))[0]

    shares = [lax.dynamic_index_in_dim(both, 1 + m * a + i, 0, keepdims=False) for i in range(m)]
    shares = list(lax.optimization_barrier(tuple(shares)))
    weight_columns = jnp.broadcast_to(w2[:, None], (2 * rows, t))
    main = [gather_cols(shares[0], order)]
    lead_own = hold(lead_all, shares, weighted, weight_columns)
    shares = [hold(x, lead_own) for x in shares[1:]]
    main += [gather_cols(x, order) for x in shares]
    lead_other = swap(lead_own, "arc")
    priors = jnp.sum(lead_own[:, rows : rows + 3].astype(F32), axis=1)
    priors = jnp.concatenate([priors[order.index(x)] for x in range(n_col)])

    if fast:
        lead_weighted, packed = lead_blocks(
            lead_own, lead_other, weight_columns, order, rows
        )
        arrived = swap(packed, "row")
        first_use = packed
    else:
        flat = jnp.concatenate([lead_own[:, :rows], lead_other[:, :rows]], axis=1)
        flat = jnp.stack([flat[order.index(x)] for x in range(n_col)])
        lead_weighted = jnp.transpose(weigh(flat, w2), (1, 0, 2)).reshape(2 * rows, width)
        first_use = lead_weighted
        half = n_col // 2
        square = jnp.einsum(
            "crt,ru->ctu",
            lax.dynamic_slice_in_dim(flat, half * a, half, 0),
            lead_weighted,
            preferred_element_type=F32,
        )
        square = lax.psum(square, "row")
        square_other = swap(square, "arc")
        square = jnp.concatenate(
            [jnp.where(first, square, square_other), jnp.where(first, square_other, square)]
        ).reshape(width, width)
        symmetric = 0.5 * (square + square.T) + jnp.diag(priors)
    rest = [gather_cols(hold(x, first_use, shares), order) for x in own[1 + 2 * m :]]

    if fast:
        return finish_fast(
            prior.reshape(kc, t),
            (packed, arrived, priors),
            (lead_own, lead_other, main, rest),
            (weighted, lead_weighted),
        )

    halves = [core_half(by_owner(x[:, :rows]), a) for x in (lead_own, lead_other)]
    split = (weighted[:rows], weighted[rows:])
    lead_split = (lead_weighted[:rows], lead_weighted[rows:])
    n_lead = partial_sums(halves, split)
    main_sums = [partial_sums([by_owner(x)], [weighted], [lead_weighted]) for x in main]
    rest_sums = [partial_sums(core_halves(by_owner(x)), split, lead_split) for x in rest]
    *_, (_, inverse) = inverse_cholesky_steps(symmetric, {})

    def sides(x):
        y = swap(x, "arc")
        return jnp.where(first, x, y), jnp.where(first, y, x)

    n_rows, p_rows = [None] * kc, [None] * kc
    n_rows[0] = jnp.concatenate(sides(n_lead[0]))
    for i, (n, p) in enumerate(main_sums):
        n_rows[1 + i], n_rows[1 + m + i] = sides(n)
        p_rows[1 + i], p_rows[1 + m + i] = sides(p)
    for i, (n, p) in enumerate(rest_sums):
        n_rows[1 + 2 * m + i] = jnp.concatenate(sides(n))
        p_rows[1 + 2 * m + i] = jnp.concatenate(sides(p))

    def in_order(x):
        x = jnp.stack(x)
        return jnp.where(r % 2 == 1, x[:, ::-1], x)

    tiles = in_order(n_rows).reshape(kc * q, t, kc, t)
    tile_rows = jnp.arange(kc * q, dtype=jnp.int32) * n_row + r
    tile_cols = jnp.arange(kc, dtype=jnp.int32) * n_col + c
    same = (tile_rows[:, None] == tile_cols[None, :]).astype(F32)
    identity = jnp.eye(t, dtype=F32)
    added = same[:, None, :, None] * identity[None, :, None, :] * prior.reshape(kc, t)[None, None]
    normal = (tiles + added).reshape(kc * q, 1, t, kc, 1, t)
    top = lax.dynamic_index_in_dim(symmetric.reshape(q, n_row, t, width), r, 1, keepdims=False)
    panel_rows = jnp.concatenate([top[None], in_order(p_rows[1:])])
    result = jnp.einsum(
        "rk,jk->rj",
        panel_rows.reshape(kc * q * t, width),
        inverse,
        precision=lax.Precision.HIGH,
        preferred_element_type=F32,
    )
    return (normal, result.reshape(kc * q, 1, t, width))


def solution(mesh):
    placed = (P(("arc", "row"), None, "col", None), P(("arc", "row")), P(None, "col", None))
    return jax.shard_map(
        body,
        mesh=mesh,
        in_specs=placed,
        out_specs=(P(None, "row", None, None, "col", None), P(None, "row", None, None)),
        check_vma=False,
    )
```

```python
import functools

import jax
import jax.numpy as jnp
from jax import lax
from jax.experimental import pallas as pl
from jax.experimental.pallas import tpu as pltpu
from jax.sharding import PartitionSpec as P

F32 = jnp.float32
BF16 = jnp.bfloat16

SHORT = pl.CostEstimate(flops=10**6, bytes_accessed=10**5, transcendentals=0)
BLOCK = 128
STRIP = 16


def dot_tn(x, y):
    return lax.dot_general(
        x, y, (((0,), (0,)), ((), ())), precision=lax.Precision.HIGHEST, preferred_element_type=F32
    )


def dot_nn(x, y):
    return jnp.dot(x, y, precision=lax.Precision.HIGHEST, preferred_element_type=F32)


def inverse_factor(square):
    n = square.shape[0]
    count = n // STRIP
    row_id = lax.broadcasted_iota(jnp.int32, (STRIP, n), 0)
    left = [square[i * STRIP : (i + 1) * STRIP, :] for i in range(count)]
    lane = lax.broadcasted_iota(jnp.int32, (STRIP, n), 1)
    right = [(lane == row_id + i * STRIP).astype(F32) for i in range(count)]
    done = []
    for b in range(count):
        ps, pe = left[b], right[b]
        columns = [
            jnp.broadcast_to(ps[:, b * STRIP + l : b * STRIP + l + 1], (STRIP, n))
            for l in range(STRIP)
        ]
        scale = jnp.zeros((STRIP, n), F32)
        for j in range(STRIP):
            rs = lax.rsqrt(columns[j][j : j + 1, :])
            col = columns[j] * rs
            below = jnp.where(row_id > j, col, 0.0)
            ps = ps - below * (ps[j : j + 1, :] * rs)
            pe = pe - below * (pe[j : j + 1, :] * rs)
            for l in range(j + 1, STRIP):
                columns[l] = columns[l] - col * (columns[l][j : j + 1, :] * rs)
            scale = jnp.where(row_id == j, rs, scale)
        ps = ps * scale
        pe = pe * scale
        done.append(pe)
        if b + 1 < count:
            update = dot_tn(ps, jnp.concatenate([ps, pe], axis=1))
            for i in range(b + 1, count):
                left[i] = left[i] - update[i * STRIP : (i + 1) * STRIP, :n]
                right[i] = right[i] - update[i * STRIP : (i + 1) * STRIP, n:]
    return jnp.concatenate(done, axis=0)


def factor_step(k, blocks, s_ref, *refs):
    lo, hi = k * BLOCK, (k + 1) * BLOCK
    u_out, e_out = refs[-2:]
    if k:
        u_ref, e_ref = refs[:2]
        above = u_ref[:, lo:hi]
        diag = s_ref[:, lo:hi] - dot_tn(above, above)
    else:
        diag = s_ref[:, lo:hi]
    inverse = inverse_factor(diag)
    width = blocks * BLOCK
    u_out[:, :hi] = jnp.zeros((BLOCK, hi), F32)
    if k + 1 < blocks:
        rest = s_ref[:, hi:]
        if k:
            rest = rest - dot_tn(above, u_ref[:, hi:])
        u_out[:, hi:] = dot_nn(inverse, rest)
        e_out[:, hi:] = jnp.zeros((BLOCK, width - hi), F32)
    if k:
        e_out[:, :lo] = -dot_nn(inverse, dot_tn(above, e_ref[:, :lo]))
    e_out[:, lo:hi] = inverse


def inverse_cholesky_steps(square, ahead):
    width = square.shape[0]
    blocks = width // BLOCK
    shape = jax.ShapeDtypeStruct((width, width), F32)
    state = None
    for k in range(blocks):
        gates = []
        if k in ahead:
            gate = after(jnp.zeros((1,), jnp.int32), *ahead[k])
            gates = [gate]
        row = pl.BlockSpec((BLOCK, width), lambda i, k=k: (k, 0))
        seen = pl.BlockSpec((k * BLOCK, width), lambda i: (0, 0))
        state = pl.pallas_call(
            functools.partial(factor_step, k, blocks),
            grid=(1,),
            out_shape=(shape, shape),
            in_specs=[row]
            + ([seen, seen] if k else [])
            + [pl.BlockSpec(memory_space=pltpu.SMEM)] * len(gates),
            out_specs=(row, row),
            input_output_aliases={1: 0, 2: 1} if k else {},
            compiler_params=pltpu.CompilerParams(vmem_limit_bytes=24 * 1024 * 1024),
            cost_estimate=SHORT,
            name=f"factor_{k}",
        )(square, *(state or ()), *gates)
        yield state


def ring_order(n, owners):
    order = []
    for owner in range(owners):
        order += list(range(owner, n, owners))[:: -1 if owner % 2 else 1]
    return order


def swap(x, axis, shift=1):
    n = lax.axis_size(axis)
    return lax.ppermute(x, axis, [(i, (i + shift) % n) for i in range(n)])


def after(index, *others):
    for x in others:
        one = lax.slice(x, (0,) * x.ndim, (1,) * x.ndim).reshape(()).astype(F32)
        index = index + jnp.minimum(jnp.abs(one), 0.0).astype(jnp.int32)
    return index


def gather_cols(x, order):
    return lax.all_gather(x, "col", axis=0, tiled=False, axis_index_groups=[order])


def weigh(x, w):
    return (x.astype(F32) * w[:, None]).astype(BF16)


def split3(x):
    hi = lax.reduce_precision(x, 8, 7)
    mid = lax.reduce_precision(x - hi, 8, 7)
    return [y.astype(BF16) for y in (hi, mid, x - hi - mid)]


def by_owner(x):
    n_row = lax.axis_size("row")
    return x.reshape((n_row, x.shape[0] // n_row) + x.shape[1:])


def product_of(blocks, owner, group):
    total = 0.0
    for x, w in zip(blocks, group):
        mine = lax.dynamic_index_in_dim(x, owner, 0, keepdims=False)
        total += jnp.einsum("qrt,ru->qtu", mine, w, preferred_element_type=F32)
    return total


def sends(blocks, groups, *wait):
    n_row = lax.axis_size("row")
    r = after(lax.axis_index("row"), *wait)
    parts = [
        [product_of(blocks, (r + d) % n_row, w).astype(BF16) for d in range(1, n_row)]
        for w in groups
    ]
    return lax.optimization_barrier(parts)


def keeps(blocks, groups, *wait):
    r = after(lax.axis_index("row"), *wait)
    return lax.optimization_barrier([product_of(blocks, r, w) for w in groups])


def receive(sent):
    return [[swap(x, "row", 1 + i) for i, x in enumerate(parts)] for parts in sent]


def partial_sums(blocks, *groups):
    totals = []
    for total, parts in zip(keeps(blocks, groups), receive(sends(blocks, groups))):
        for x in parts:
            total = total + x.astype(F32)
        totals.append(total)
    return totals


def core_half(x, core):
    half = x.shape[1] // 2
    return lax.dynamic_slice_in_dim(x, half * core, half, 1)


def core_halves(x):
    a = lax.axis_index("arc")
    return [core_half(x, a), swap(core_half(x, 1 - a), "arc")]


PAIRS = (((0, 0), (0, 1), (0, 2), (0, 3), (3, 3)), ((1, 1), (1, 2), (1, 3), (2, 2), (2, 3)))
WIDE = 256


def lead_kernel(order, rows, pairs_ref, own_ref, other_ref, w_ref, weighted_ref, s_ref, flat_ref):
    @pl.when(pl.program_id(0) == 0)
    def _():
        t = own_ref.shape[2]
        for pos, c in enumerate(order):
            for arc, ref in enumerate((own_ref, other_ref)):
                x = ref[pos, :rows, :]
                place = (pl.ds(arc * rows, rows), pl.ds(c * t, t))
                flat_ref[place] = x
                weighted_ref[place] = (x.astype(F32) * w_ref[pl.ds(arc * rows, rows), :]).astype(BF16)

    def columns(entry):
        return pl.ds(pl.multiple_of(pairs_ref[2 * pl.program_id(0) + entry] * WIDE, WIDE), WIDE)

    def product(x, y):
        return lax.dot_general(x, y, (((0,), (0,)), ((), ())), preferred_element_type=F32)

    i, j = columns(0), columns(1)
    s_ref[0] = 0.5 * (
        product(flat_ref[:, i], weighted_ref[:, j]) + product(weighted_ref[:, i], flat_ref[:, j])
    )


def lead_blocks(own, other, weight_columns, order, rows):
    n, padded, t = own.shape
    width = n * t
    count = len(PAIRS[0])
    pairs = jnp.array(PAIRS, jnp.int32).reshape(2, 2 * count)[lax.axis_index("arc")]
    whole = pl.BlockSpec((n, padded, t), lambda s, p: (0, 0, 0))
    return pl.pallas_call(
        functools.partial(lead_kernel, order, rows),
        grid_spec=pltpu.PrefetchScalarGridSpec(
            num_scalar_prefetch=1,
            grid=(count,),
            in_specs=[whole, whole, pl.BlockSpec((2 * rows, t), lambda s, p: (0, 0))],
            out_specs=(
                pl.BlockSpec((2 * rows, width), lambda s, p: (0, 0)),
                pl.BlockSpec((1, WIDE, WIDE), lambda s, p: (s, 0, 0)),
            ),
            scratch_shapes=[pltpu.VMEM((2 * rows, width), BF16)],
        ),
        out_shape=(
            jax.ShapeDtypeStruct((2 * rows, width), BF16),
            jax.ShapeDtypeStruct((count, WIDE, WIDE), F32),
        ),
        compiler_params=pltpu.CompilerParams(vmem_limit_bytes=52 * 1024 * 1024),
        cost_estimate=SHORT,
        name="lead_blocks",
    )(pairs, own, other, weight_columns)


def assemble_kernel(table_ref, mine_ref, theirs_ref, late_ref, late_other_ref, prior_ref, out_ref):
    i, j = pl.program_id(0), pl.program_id(1)
    entry = table_ref[4 * i + j]
    at = entry % 8
    block = jnp.where(entry < 8, mine_ref[at] + late_ref[at], theirs_ref[at] + late_other_ref[at])

    @pl.when(i < j)
    def _():
        out_ref[...] = block

    @pl.when(i > j)
    def _():
        out_ref[...] = block.T

    @pl.when(i == j)
    def _():
        x = lax.broadcasted_iota(jnp.int32, block.shape, 0)
        y = lax.broadcasted_iota(jnp.int32, block.shape, 1)
        out_ref[...] = block + jnp.where(x == y, prior_ref[...], 0.0)


def assemble(mine, theirs, late, late_other, priors, *wait):
    width = priors.shape[0]
    tables = [[0] * 16, [0] * 16]
    for core in range(2):
        for slot, (i, j) in enumerate(PAIRS[core]):
            for a in range(2):
                tables[a][4 * i + j] = tables[a][4 * j + i] = slot + (0 if a == core else 8)
    table = after(jnp.array(tables, jnp.int32)[lax.axis_index("arc")], *wait)
    blocks = pl.BlockSpec(mine.shape, lambda i, j, p: (0, 0, 0))
    return pl.pallas_call(
        assemble_kernel,
        grid_spec=pltpu.PrefetchScalarGridSpec(
            num_scalar_prefetch=1,
            grid=(4, 4),
            in_specs=[blocks] * 4 + [pl.BlockSpec((1, WIDE), lambda i, j, p: (0, j))],
            out_specs=pl.BlockSpec((WIDE, WIDE), lambda i, j, p: (i, j)),
        ),
        out_shape=jax.ShapeDtypeStruct((width, width), F32),
        compiler_params=pltpu.CompilerParams(vmem_limit_bytes=24 * 1024 * 1024),
        cost_estimate=SHORT,
        name="assemble",
    )(table, mine, theirs, late, late_other, priors[None])


def finish_kernel(top, halved, kc, q, n_row, base, step, here_ref, *refs):
    sums, refs = refs[:4], refs[4:]
    if top:
        square_ref, refs = refs[0], refs[1:]
    hi_ref, lo_ref, prior_ref = refs[:3]
    normal_ref, panel_ref, parts = refs[-3:]
    a, r, c = here_ref[0], here_ref[1], here_ref[2]
    g = pl.program_id(0)
    t = prior_ref.shape[1]
    k = base + step * g
    odd = r % 2
    size = q * t
    x = lax.broadcasted_iota(jnp.int32, (t, t), 0)
    y = lax.broadcasted_iota(jnp.int32, (t, t), 1)

    for z in range(q):
        at = jnp.where(odd == 1, q - 1 - z, z)
        core, index = (at // (q // 2), at % (q // 2)) if halved else (g, at)
        use = core == a

        def total(columns):
            keep, keep_other, late, late_other = [ref[index, :, columns] for ref in sums]
            return jnp.where(use, keep, keep_other) + jnp.where(use, late, late_other).astype(F32)

        rows = total(slice(0, kc * t))
        for k2 in range(kc):
            tile = rows[:, k2 * t : (k2 + 1) * t]
            same = jnp.logical_and(k == k2, c == z * n_row + r)
            tile = tile + jnp.where(jnp.logical_and(same, x == y), prior_ref[k2 : k2 + 1, :], 0.0)
            normal_ref[pl.ds(z * t * kc + k2, t, stride=kc), :] = tile
        if top:
            first = pl.multiple_of((z * n_row + r) * t, t)
            rows = square_ref[pl.ds(first, t), :]
        else:
            rows = total(slice(kc * t, None))
        high = rows.astype(BF16)
        parts[z * t : (z + 1) * t, :] = high
        parts[size + z * t : size + (z + 1) * t, :] = (rows - high.astype(F32)).astype(BF16)

    def product(u, v):
        return lax.dot_general(u, v, (((1,), (1,)), ((), ())), preferred_element_type=F32)

    width = panel_ref.shape[1]
    for lo in range(0, width, WIDE):
        hi = lo + WIDE
        both = product(parts[:, :hi], hi_ref[lo:hi, :hi])
        panel_ref[:, lo:hi] = (
            both[:size] + both[size:] + product(parts[:size, :hi], lo_ref[lo:hi, :hi])
        )


def finish(outputs, here, sums, square, inverse, prior, halved, base, step, count, kc, q, n_row):
    t = prior.shape[1]
    width = inverse[0].shape[0]
    top = len(square) == 1
    arrays = [*sums, *square, *inverse, prior]

    def spec(x):
        if x.ndim == 3:
            return pl.BlockSpec(x.shape, lambda g, p: (0, 0, 0), pipeline_mode=pl.Buffered(1))
        return pl.BlockSpec(x.shape, lambda g, p: (0, 0), pipeline_mode=pl.Buffered(1))

    shapes = (
        jax.ShapeDtypeStruct((kc * q * t * kc, t), F32),
        jax.ShapeDtypeStruct((kc * q * t, width), F32),
    )
    n_in = 1 + len(arrays)

    def place(g, p):
        return (base + step * g, 0)

    return pl.pallas_call(
        functools.partial(finish_kernel, top, halved, kc, q, n_row, base, step),
        grid_spec=pltpu.PrefetchScalarGridSpec(
            num_scalar_prefetch=1,
            grid=(count,),
            in_specs=[spec(x) for x in arrays] + [pl.BlockSpec(memory_space=pl.ANY)] * len(outputs),
            out_specs=(pl.BlockSpec((q * t * kc, t), place), pl.BlockSpec((q * t, width), place)),
            scratch_shapes=[pltpu.VMEM((2 * q * t, width), BF16)],
        ),
        out_shape=shapes,
        input_output_aliases={n_in: 0, n_in + 1: 1} if outputs else {},
        compiler_params=pltpu.CompilerParams(vmem_limit_bytes=32 * 1024 * 1024),
        cost_estimate=pl.CostEstimate(
            flops=count * 6 * 10**9, bytes_accessed=count * 8 * 10**6, transcendentals=0
        ),
        name=f"finish_{base}",
    )(here, *arrays, *outputs)


def finish_fast(prior, leading, gathered, weights):
    packed, arrived, priors = leading
    lead_own, lead_other, main, rest = gathered
    kc, t = prior.shape
    n_row = lax.axis_size("row")
    q = lax.axis_size("col") // n_row
    m = len(main)
    a, r, c = [lax.axis_index(x) for x in ("arc", "row", "col")]
    here = jnp.stack([a, r, c]).astype(jnp.int32)
    half = q // 2

    def pair(x):
        return [x, swap(x, "arc")]

    def rows_of(keep, late):
        return pair(keep) + pair(late)

    wide = lax.optimization_barrier(jnp.concatenate(weights, axis=1))
    rows = wide.shape[0] // 2
    other_owner = (r + 1) % n_row

    def product(blocks, place, w, dtype, *wait):
        x = lax.dynamic_index_in_dim(blocks, after(place, *wait), 0, keepdims=False)
        total = jnp.einsum("qrt,ru->qtu", x, w, preferred_element_type=F32)
        return lax.optimization_barrier(total.astype(dtype))

    def half_products(own, other, w, *wait):
        mine = core_half(by_owner(own), after(a, *wait))
        x = jnp.concatenate([mine[:, :, :rows], other[:, :, :rows]], axis=2)
        total = jnp.einsum("oqrt,ru->oqtu", x, w, preferred_element_type=F32)
        total = lax.optimization_barrier(total)
        send = lax.dynamic_index_in_dim(total, other_owner, 0, keepdims=False).astype(BF16)
        return send, lax.dynamic_index_in_dim(total, r, 0, keepdims=False)

    x = core_half(by_owner(lead_other), a)
    lead_sent, lead_keep = half_products(lead_own, x, wide[:, : kc * t], packed)
    lead_late = swap(lead_sent, "row")
    main = [by_owner(x) for x in main]
    arrived = arrived + after(jnp.int32(0), lead_keep).astype(F32)
    blocks = pair(packed) + pair(arrived)
    sent = product(main[0], other_owner, wide, BF16, lead_keep, lead_late, blocks[3])
    late = [swap(sent, "row")]
    symmetric = assemble(*blocks, priors, sent)

    ahead = {7: late}
    for state in inverse_cholesky_steps(symmetric, ahead):
        pass
    high = lax.reduce_precision(state[1], 8, 7)
    inverse = (high.astype(BF16), (state[1] - high).astype(BF16))
    inverse = lax.optimization_barrier(inverse)

    wait = inverse[1]
    for i in range(1, m):
        wait = product(main[i], other_owner, wide, BF16, wait)
        late.append(swap(wait, "row"))
    kept = [product(main[0], r, wide, F32, wait)]
    args = (inverse, prior)
    shape = (kc, q, n_row)
    gate = after(here, kept[0])
    out = finish([], gate, rows_of(lead_keep, lead_late), [symmetric], *args, True, 0, 1, 1, *shape)
    wait = out[1]
    for i in range(1, m):
        wait = product(main[i], r, wide, F32, wait)
        kept.append(wait)
    rest_kept = []
    for x in rest:
        received = swap(core_half(by_owner(x), after(1 - a, wait)), "arc")
        zero = after(jnp.int32(0), received).astype(BF16)
        late[1:m] = [y + zero for y in late[1:m]]
        sent, keep = half_products(x, received, wide, wait, *late[1:m])
        late.append(swap(sent, "row"))
        rest_kept.append(keep)
        wait = sent
    gate = after(here, wait)
    out = finish(out, gate, rows_of(kept[0], late[0]), [], *args, False, 1, m, 2, *shape)
    for i in range(1, m):
        out = finish(out, gate, rows_of(kept[i], late[i]), [], *args, False, 1 + i, m, 2, *shape)
    zero = after(jnp.int32(0), out[1]).astype(BF16)
    for i, (keep, x) in enumerate(zip(rest_kept, late[m:])):
        sums = rows_of(keep, x + zero)
        out = finish(out, gate, sums, [], *args, True, 1 + 2 * m + i, 1, 1, *shape)
    normal, panel = out
    return (normal.reshape(kc * q, 1, t, kc, 1, t), panel.reshape(kc * q, 1, t, -1))


def body(design, obs_weight, prior):
    n_row = lax.axis_size("row")
    n_col = lax.axis_size("col")
    a = lax.axis_index("arc")
    r = lax.axis_index("row")
    c = lax.axis_index("col")
    rows, kc, _, t = design.shape
    q = n_col // n_row
    m = (kc - 1) // 2
    width = n_col * t
    first = a == 0
    fast = t == 128 and width == 4 * WIDE and n_row == 2
    order = ring_order(n_col, n_row)
    own = lax.optimization_barrier(jnp.transpose(design[:, :, 0, :], (1, 0, 2)))

    extra = jnp.concatenate([p[None] for p in split3(prior[0, 0])] + [jnp.zeros((13, t), BF16)])
    lead_in = lax.pad(design[:, 0, 0, :], BF16(0), ((0, 16, 0), (0, 0, 0)))
    lead_in = lead_in + lax.pad(extra, BF16(0), ((rows, 0, 0), (0, 0, 0)))
    lead_all = gather_cols(lead_in, order)
    other = swap(own, "arc")
    weight_other = swap(obs_weight, "arc")
    both = jnp.concatenate([own, other], axis=1)
    w2 = jnp.concatenate([obs_weight, weight_other])
    weighted = jnp.transpose(weigh(both, w2), (1, 0, 2)).reshape(2 * rows, kc * t)
    weighted = lax.optimization_barrier(weighted)

    def hold(x, *others):
        return lax.optimization_barrier((x, others))[0]

    shares = [lax.dynamic_index_in_dim(both, 1 + m * a + i, 0, keepdims=False) for i in range(m)]
    shares = list(lax.optimization_barrier(tuple(shares)))
    weight_columns = jnp.broadcast_to(w2[:, None], (2 * rows, t))
    main = [gather_cols(shares[0], order)]
    lead_own = hold(lead_all, shares, weighted, weight_columns)
    shares = [hold(x, lead_own) for x in shares[1:]]
    main += [gather_cols(x, order) for x in shares]
    lead_other = swap(lead_own, "arc")
    priors = jnp.sum(lead_own[:, rows : rows + 3].astype(F32), axis=1)
    priors = jnp.concatenate([priors[order.index(x)] for x in range(n_col)])

    if fast:
        lead_weighted, packed = lead_blocks(
            lead_own, lead_other, weight_columns, order, rows
        )
        arrived = swap(packed, "row")
        first_use = packed
    else:
        flat = jnp.concatenate([lead_own[:, :rows], lead_other[:, :rows]], axis=1)
        flat = jnp.stack([flat[order.index(x)] for x in range(n_col)])
        lead_weighted = jnp.transpose(weigh(flat, w2), (1, 0, 2)).reshape(2 * rows, width)
        first_use = lead_weighted
        half = n_col // 2
        square = jnp.einsum(
            "crt,ru->ctu",
            lax.dynamic_slice_in_dim(flat, half * a, half, 0),
            lead_weighted,
            preferred_element_type=F32,
        )
        square = lax.psum(square, "row")
        square_other = swap(square, "arc")
        square = jnp.concatenate(
            [jnp.where(first, square, square_other), jnp.where(first, square_other, square)]
        ).reshape(width, width)
        symmetric = 0.5 * (square + square.T) + jnp.diag(priors)
    rest = [gather_cols(hold(x, first_use, shares), order) for x in own[1 + 2 * m :]]

    if fast:
        return finish_fast(
            prior.reshape(kc, t),
            (packed, arrived, priors),
            (lead_own, lead_other, main, rest),
            (weighted, lead_weighted),
        )

    halves = [core_half(by_owner(x[:, :rows]), a) for x in (lead_own, lead_other)]
    split = (weighted[:rows], weighted[rows:])
    lead_split = (lead_weighted[:rows], lead_weighted[rows:])
    n_lead = partial_sums(halves, split)
    main_sums = [partial_sums([by_owner(x)], [weighted], [lead_weighted]) for x in main]
    rest_sums = [partial_sums(core_halves(by_owner(x)), split, lead_split) for x in rest]
    *_, (_, inverse) = inverse_cholesky_steps(symmetric, {})

    def sides(x):
        y = swap(x, "arc")
        return jnp.where(first, x, y), jnp.where(first, y, x)

    n_rows, p_rows = [None] * kc, [None] * kc
    n_rows[0] = jnp.concatenate(sides(n_lead[0]))
    for i, (n, p) in enumerate(main_sums):
        n_rows[1 + i], n_rows[1 + m + i] = sides(n)
        p_rows[1 + i], p_rows[1 + m + i] = sides(p)
    for i, (n, p) in enumerate(rest_sums):
        n_rows[1 + 2 * m + i] = jnp.concatenate(sides(n))
        p_rows[1 + 2 * m + i] = jnp.concatenate(sides(p))

    def in_order(x):
        x = jnp.stack(x)
        return jnp.where(r % 2 == 1, x[:, ::-1], x)

    tiles = in_order(n_rows).reshape(kc * q, t, kc, t)
    tile_rows = jnp.arange(kc * q, dtype=jnp.int32) * n_row + r
    tile_cols = jnp.arange(kc, dtype=jnp.int32) * n_col + c
    same = (tile_rows[:, None] == tile_cols[None, :]).astype(F32)
    identity = jnp.eye(t, dtype=F32)
    added = same[:, None, :, None] * identity[None, :, None, :] * prior.reshape(kc, t)[None, None]
    normal = (tiles + added).reshape(kc * q, 1, t, kc, 1, t)
    top = lax.dynamic_index_in_dim(symmetric.reshape(q, n_row, t, width), r, 1, keepdims=False)
    panel_rows = jnp.concatenate([top[None], in_order(p_rows[1:])])
    result = jnp.einsum(
        "rk,jk->rj",
        panel_rows.reshape(kc * q * t, width),
        inverse,
        precision=lax.Precision.HIGH,
        preferred_element_type=F32,
    )
    return (normal, result.reshape(kc * q, 1, t, width))


def solution(mesh):
    placed = (P(("arc", "row"), None, "col", None), P(("arc", "row")), P(None, "col", None))
    return jax.shard_map(
        body,
        mesh=mesh,
        in_specs=placed,
        out_specs=(P(None, "row", None, None, "col", None), P(None, "row", None, None)),
        check_vma=False,
    )
```
